128 devices in a mesh: sub: 16 (over y, z), cont: 8 (over x, core).
Axes of the slice: x: 4, y: 4, z: 4, core: 2. Of those that a mesh axis runs over, the one named last changes fastest.
Arguments:
- schur_matrix: float32 [16, 8, 1536, 1536], P('sub', 'cont'), as said below
- load_vectors: float32 [16, 8, 1536, 512], P('sub', 'cont')
- glue_blocks: int32 [16, 8, 8], P('sub', 'cont'), may hold values from 0 to 7, each once within a row
- contact_order: int32 [16, 8, 8], P('sub', 'cont'), may hold values from 0 to 7, each once within a row
- active_flags: int32 [16, 8, 512], P('sub', 'cont'), may hold values 0 or 1
Outputs:
- glue_multipliers: float32 [16, 8, 512, 512], P('sub', 'cont')
- contact_multipliers: float32 [16, 8, 512, 512], P('sub', 'cont')
- glue_residual: float32 [16, 8, 512, 512], P('sub', 'cont')
- contact_residual: float32 [16, 8, 512, 512], P('sub', 'cont')
The draws below stay inside these ranges and needn't reach their ends.
Inputs may be any that keep to these rules, and one draw needn't show every extreme that they name: `glue_blocks`: each row lists the 8 upper-face blocks once each. `contact_order`: each row lists the 8 contact blocks once each. `schur_matrix`: every tile is symmetric and positive definite.
All inputs are finite; a program needn't handle non-finite values. No bound on the sum of `active_flags` on one device may be relied on, other than what follows from the above.
Results may differ from the reference program's by a relative error of at most 0.0003.
Values sent between devices are 32-bit elements; how exact they have to be, the bound alone decides.
A program may use at most 128 MiB of HBM per device.

```python
import math
import jax
import jax.numpy as jnp
from jax import lax

BLOCK = 64
FACE_BLOCKS = 8
CONT_BLOCKS = 8
IFACE = 1536
LOADS = 512
ITERS = 2
SUB_ROWS = 16
SUB_COLS = 8
CDOF = 512


def draw_schur_matrix(key, part):
    tile_keys = jax.random.split(key, SUB_ROWS * SUB_COLS)

    def one_tile(tile_key):
        factor_key, shift_key = jax.random.split(tile_key)
        factor = jax.random.truncated_normal(factor_key, -4.0, 4.0, (IFACE, IFACE), jnp.float32)
        shift = jax.random.uniform(shift_key, (IFACE,), jnp.float32, 0.3, 1.0)
        gram = jnp.dot(factor, factor.T, precision=lax.Precision.HIGHEST) * (1.0 / IFACE)
        gram = 0.5 * (gram + gram.T)
        identity_mat = jnp.eye(IFACE, dtype=jnp.float32)
        return gram + identity_mat * shift[:, None]
    tiles = lax.map(one_tile, tile_keys)
    return tiles.reshape(SUB_ROWS, SUB_COLS, IFACE, IFACE)


def draw_load_vectors(key, part):
    noise_key, scale_key = jax.random.split(key)
    shape_all = (SUB_ROWS, SUB_COLS, IFACE, LOADS)
    noise_vals = jax.random.truncated_normal(noise_key, -5.0, 5.0, shape_all, jnp.float32)
    row_scale = jnp.exp(jax.random.uniform(scale_key, (SUB_ROWS, SUB_COLS, IFACE, 1), jnp.float32, math.log(0.3), math.log(3.0)))
    position = jnp.arange(SUB_ROWS, dtype=jnp.float32).reshape(SUB_ROWS, 1, 1, 1)
    rising = 1.0 + 2.0 * position / max(SUB_ROWS - 1, 1)
    return noise_vals * row_scale * rising


def with_ends(drawn, key, least, top_value):
    index_at = [jax.random.randint(jax.random.fold_in(key, axis), (), 0, length) for axis, length in enumerate(drawn.shape)]
    longest = drawn.shape.index(max(drawn.shape))
    beside = index_at[:longest] + [(index_at[longest] + 1) % drawn.shape[longest]] + index_at[longest + 1:]
    return drawn.at[tuple(index_at)].set(least).at[tuple(beside)].set(top_value)


def setup_inputs(seed: int = 0) -> dict:
    seeds = jax.random.split(jax.random.key(seed), 6)
    schur_matrix = draw_schur_matrix(jax.random.fold_in(seeds[5], 71), 0)
    load_vectors = draw_load_vectors(jax.random.fold_in(seeds[5], 71), 0)
    glue_blocks = jax.vmap(lambda own: jax.random.permutation(own, FACE_BLOCKS))(jax.random.split(seeds[2], SUB_ROWS * SUB_COLS)).reshape((SUB_ROWS, SUB_COLS, FACE_BLOCKS)).astype(jnp.int32)
    contact_order = jax.vmap(lambda own: jax.random.permutation(own, CONT_BLOCKS))(jax.random.split(seeds[3], SUB_ROWS * SUB_COLS)).reshape((SUB_ROWS, SUB_COLS, CONT_BLOCKS)).astype(jnp.int32)
    active_flags = with_ends((jax.random.randint(seeds[4], (SUB_ROWS, SUB_COLS, CDOF), 0, 4) < 3).astype(jnp.int32), jax.random.fold_in(seeds[4], 1), 0, 1)
    return dict(schur_matrix=schur_matrix, load_vectors=load_vectors, glue_blocks=glue_blocks, contact_order=contact_order, active_flags=active_flags)


precise = lax.Precision.HIGHEST


def one_hot_rows(indices, count):
    return (indices[..., :, None] == jnp.arange(count, dtype=jnp.int32)).astype(jnp.float32)


def reference_jump(fields, glue_hot, order_hot):
    blocks = fields.reshape(SUB_ROWS, SUB_COLS, -1, BLOCK, LOADS)
    lower_face = blocks[:, :, :FACE_BLOCKS]
    upper_face = blocks[:, :, FACE_BLOCKS:2 * FACE_BLOCKS]
    contact = blocks[:, :, 2 * FACE_BLOCKS:]
    upper_prev = jnp.concatenate([jnp.zeros_like(upper_face[:1]), upper_face[:-1]], axis=0)
    glue_jump = lower_face - jnp.einsum("ijkm,ijmxr->ijkxr", glue_hot, upper_prev, precision=precise)
    sent_blocks = jnp.einsum("ijpk,ijkxr->ijpxr", order_hot, contact, precision=precise)
    grouped = sent_blocks.reshape(SUB_ROWS, SUB_COLS, SUB_COLS, -1, BLOCK, LOADS)
    buckets = jnp.transpose(grouped, (0, 2, 1, 3, 4, 5)).reshape(SUB_ROWS, SUB_COLS, -1, LOADS)
    return glue_jump.reshape(SUB_ROWS, SUB_COLS, -1, LOADS), buckets


def reference_spread(glue_vals, bucket_vals, glue_hot, order_hot):
    lower_face = glue_vals.reshape(SUB_ROWS, SUB_COLS, FACE_BLOCKS, BLOCK, LOADS)
    passed = jnp.einsum("ijkm,ijkxr->ijmxr", glue_hot, lower_face, precision=precise)
    upper_face = -jnp.concatenate([passed[1:], jnp.zeros_like(passed[:1])], axis=0)
    grouped = bucket_vals.reshape(SUB_ROWS, SUB_COLS, SUB_COLS, -1, BLOCK, LOADS)
    sent_blocks = jnp.transpose(grouped, (0, 2, 1, 3, 4, 5)).reshape(SUB_ROWS, SUB_COLS, CONT_BLOCKS, BLOCK, LOADS)
    contact = jnp.einsum("ijpk,ijpxr->ijkxr", order_hot, sent_blocks, precision=precise)
    whole = jnp.concatenate([lower_face, upper_face, contact], axis=2)
    return whole.reshape(SUB_ROWS, SUB_COLS, -1, LOADS)


def apply_schur(schur_matrix, fields):
    return jnp.einsum("ijab,ijbr->ijar", schur_matrix, fields, precision=precise)


def column_dots(left_vec, right_vec):
    return jnp.sum(left_vec[0] * right_vec[0], axis=(0, 1, 2)) + jnp.sum(left_vec[1] * right_vec[1], axis=(0, 1, 2))


def combine(left_vec, scaling, right_vec):
    return (left_vec[0] + scaling * right_vec[0], left_vec[1] + scaling * right_vec[1])


def reference(schur_matrix, load_vectors, glue_blocks, contact_order, active_flags):
    glue_hot = one_hot_rows(glue_blocks, FACE_BLOCKS)
    order_hot = one_hot_rows(contact_order, CONT_BLOCKS)
    keep_mask = active_flags.astype(jnp.float32)[..., None]

    def operate(direction):
        fields = reference_spread(direction[0], direction[1], glue_hot, order_hot)
        glue_jump, bucket_jump = reference_jump(apply_schur(schur_matrix, fields), glue_hot, order_hot)
        return (glue_jump, bucket_jump * keep_mask)

    glue_rhs, bucket_rhs = reference_jump(apply_schur(schur_matrix, load_vectors), glue_hot, order_hot)
    residual = (glue_rhs, bucket_rhs * keep_mask)
    direction = residual
    multipliers = (jnp.zeros_like(residual[0]), jnp.zeros_like(residual[1]))
    norm_now = column_dots(residual, residual)
    for iteration in range(ITERS):
        product_vec = operate(direction)
        step_alpha = norm_now / column_dots(direction, product_vec)
        multipliers = combine(multipliers, step_alpha, direction)
        residual = combine(residual, -step_alpha, product_vec)
        if iteration + 1 < ITERS:
            norm_next = column_dots(residual, residual)
            direction = combine(residual, norm_next / norm_now, direction)
            norm_now = norm_next
    return multipliers[0], multipliers[1], residual[0], residual[1]
```

```python
import jax
import jax.numpy as jnp
from jax import lax
from jax.experimental import pallas as pl
from jax.experimental.pallas import tpu as pltpu
from jax.sharding import PartitionSpec as P

BLOCK = 64
NBLK = 8
FACE = BLOCK * NBLK
IFACE = 3 * FACE
LOADS = 512
CHUNKS = 2
COLS = LOADS // CHUNKS
STEPS = 3 * CHUNKS
F32 = jnp.float32
BF16 = jnp.bfloat16


def fold(x):
    return jnp.sum(x.reshape(x.shape[0] // 8, 8, COLS), axis=0)


def row_sum(x):
    return jnp.sum(x, axis=0, keepdims=True)


def kernel(
    rows, cols,
    schur, loads, glue, order, flags,
    out_gm, out_cm, out_gr, out_cr,
    stage_s, s_hi, s_lo, field, f_hi, f_lo, prod, first, mask,
    low_out, con_out, up_in_0, up_in_1, up_in_2, up_in_3, up_in_4, up_in_5, low_in, con_in, flag_in, flag_own,
    sum_own, sum_sub, part_own, sum_con, result, inverse,
    s_sem, l_sem, o_sem,
    up_ss, up_rs, low_ss, low_rs, con_ss, con_rs, flag_ss, flag_rs, sub_ss, sub_rs, cont_ss, cont_rs,
):
    up_in = (up_in_0, up_in_1, up_in_2, up_in_3, up_in_4, up_in_5)
    i = lax.axis_index("sub")
    j = lax.axis_index("cont")
    after = lax.rem(i + 1, rows)
    before = lax.rem(i + rows - 1, rows)
    has_before = i > 0
    has_after = i < rows - 1

    barrier = pltpu.get_barrier_semaphore()
    for k in range(1, rows):
        pl.semaphore_signal(barrier, 1, device_id={"sub": lax.rem(i + k, rows)})
    for k in range(1, cols):
        pl.semaphore_signal(barrier, 1, device_id={"cont": lax.rem(j + k, cols)})

    def load_copy(c):
        return pltpu.make_async_copy(loads.at[:, pl.ds(c * COLS, COLS)], field.at[c], l_sem.at[c])

    def schur_copy(r, slot):
        return pltpu.make_async_copy(schur.at[pl.ds(r, FACE)], stage_s.at[slot], s_sem.at[slot])

    load_copy(0).start()
    schur_copy(FACE, 0).start()
    schur_copy(0, 1).start()
    schur_copy(2 * FACE, 2).start()
    for c in range(1, CHUNKS):
        load_copy(c).start()

    def up_copy(s):
        return pltpu.make_async_remote_copy(
            prod.at[s, pl.ds(NBLK, NBLK)], up_in[s], up_ss.at[s], up_rs.at[s], device_id={"sub": after})

    def low_copy(s):
        return pltpu.make_async_remote_copy(
            low_out.at[s], low_in.at[s], low_ss.at[s], low_rs.at[s], device_id={"sub": before})

    def con_copy(s, k):
        t = lax.rem(j + k, cols)
        return pltpu.make_async_remote_copy(
            con_out.at[s, t], con_in.at[s, j], con_ss.at[s, k], con_rs.at[s, k], device_id={"cont": t})

    def flag_copy(k):
        return pltpu.make_async_remote_copy(
            flag_own, flag_in.at[j], flag_ss.at[k], flag_rs.at[k], device_id={"cont": lax.rem(j + k, cols)})

    def sub_copy(a, k):
        return pltpu.make_async_remote_copy(
            sum_own.at[a], sum_sub.at[a, i], sub_ss.at[a, k], sub_rs.at[a, k], device_id={"sub": lax.rem(i + k, rows)})

    def cont_copy(a, k):
        return pltpu.make_async_remote_copy(
            part_own.at[a], sum_con.at[a, j], cont_ss.at[a, k], cont_rs.at[a, k], device_id={"cont": lax.rem(j + k, cols)})

    for n, ref in enumerate((glue, order)):
        for m in range(NBLK):
            found = jnp.int32(0)
            for k in range(1, NBLK):
                found = jnp.maximum(found, k * (ref[0, k] == m).astype(jnp.int32))
            inverse[n, m] = found

    def split_store(r, x):
        hi = x.astype(BF16)
        f_hi[pl.ds(r, x.shape[0]), :] = hi
        f_lo[pl.ds(r, x.shape[0]), :] = (x - hi.astype(F32)).astype(BF16)

    def product(s, r):
        a_hi = s_hi[pl.ds(r, FACE), :]
        a_lo = s_lo[pl.ds(r, FACE), :]
        value = jnp.dot(a_hi, f_hi[...], preferred_element_type=F32)
        value = value + jnp.dot(a_hi, f_lo[...], preferred_element_type=F32)
        value = value + jnp.dot(a_lo, f_hi[...], preferred_element_type=F32)
        prod[s, pl.ds(lax.div(r, BLOCK), NBLK)] = value.reshape(NBLK, BLOCK, COLS)
        return value

    def group_row(g):
        return pl.multiple_of(jnp.where(g == 0, FACE, jnp.where(g == 1, 0, 2 * FACE)), FACE)

    def send_up(s):
        up_copy(s).start()

    def send_low(s):
        def move(m, _):
            low_out[s, m] = prod[s, inverse[0, m]]
            return 0
        lax.fori_loop(0, NBLK, move, 0)
        low_copy(s).start()

    def send_contact(s):
        def move(t, _):
            con_out[s, t] = prod[s, 2 * NBLK + order[0, t]] * mask[t]
            return 0
        lax.fori_loop(0, NBLK, move, 0)
        for k in range(1, cols):
            con_copy(s, k).start()
        con_in[s, j] = con_out[s, j]

    def glue_part(s, k):
        return prod[s, k] - jnp.where(has_before, up_in[s][glue[0, k]], 0.0)

    def upper_part(s, m):
        return jnp.where(has_after, prod[s, NBLK + m] - low_in[s, m], 0.0)

    def contact_part(s, k):
        return prod[s, 2 * NBLK + k] * mask[inverse[1, k]]

    def start_sum(a, values):
        for n, v in enumerate(values):
            sum_own[a, n] = v
            sum_sub[a, i, n] = v
        for k in range(1, rows):
            sub_copy(a, k).start()

    def pass_sum(a, count):
        for k in range(1, rows):
            sub_copy(a, k).wait_recv()
        for n in range(count):
            v = sum_sub[a, 0, n]
            for k in range(1, rows):
                v = v + sum_sub[a, k, n]
            part_own[a, n] = v
            sum_con[a, j, n] = v
        for k in range(1, cols):
            cont_copy(a, k).start()

    def end_sum(a, count):
        for k in range(1, cols):
            cont_copy(a, k).wait_recv()
        totals = []
        for n in range(count):
            v = sum_con[a, 0, n]
            for k in range(1, cols):
                v = v + sum_con[a, k, n]
            totals.append(v)
        return totals

    zero8 = jnp.zeros((8, COLS), F32)
    zero1 = jnp.zeros((1, COLS), F32)

    for c in range(CHUNKS):
        s = c
        load_copy(c).wait()

        def part(n, _):
            r = pl.multiple_of(n * 128, 128)
            split_store(r, field[c, pl.ds(r, 128), :])
            return 0
        lax.fori_loop(0, IFACE // 128, part, 0)

        def group(g, _):
            r = group_row(g)
            if c == 0:
                schur_copy(r, g).wait()
                x = stage_s[g]
                hi = x.astype(BF16)
                s_hi[pl.ds(r, FACE), :] = hi
                s_lo[pl.ds(r, FACE), :] = (x - hi.astype(F32)).astype(BF16)
            product(s, r)
            if c == 0:
                @pl.when(g == 0)
                def _():
                    pl.semaphore_wait(barrier, rows - 1 + cols - 1)
                    up_copy(0).start()

                @pl.when(g == 1)
                def _():
                    send_low(0)
            return 0
        lax.fori_loop(0, 3, group, 0)
        if c == 0:
            flag_own[...] = flags[...].astype(F32)
            for k in range(1, cols):
                flag_copy(k).start()
            flag_in[j] = flag_own[...]
        else:
            send_up(s)
            send_low(s)

    for k in range(1, cols):
        flag_copy(k).wait_recv()
    lane = lax.broadcasted_iota(jnp.int32, (BLOCK, FACE), 1)
    want = lax.broadcasted_iota(jnp.int32, (BLOCK, FACE), 0) + j * BLOCK

    def mask_of(t, _):
        picked = jnp.where(lane == want, flag_in[t], 0.0)
        mask[t] = jnp.broadcast_to(jnp.sum(picked, axis=1, keepdims=True), (BLOCK, COLS))
        return 0
    lax.fori_loop(0, NBLK, mask_of, 0)

    norms0 = []
    for c in range(CHUNKS):
        was, s = c, CHUNKS + c
        send_contact(was)
        up_copy(was).wait_recv()
        low_copy(was).wait_recv()

        def part(k, norm):
            r = pl.multiple_of(k * BLOCK, BLOCK)
            x = glue_part(was, k)
            norm = norm + fold(x * x)
            field[c, pl.ds(r, BLOCK), :] = x
            split_store(r, x)
            x = upper_part(was, k)
            field[c, pl.ds(pl.multiple_of(FACE + r, BLOCK), BLOCK), :] = x
            split_store(pl.multiple_of(FACE + r, BLOCK), x)
            x = contact_part(was, k)
            norm = norm + fold(x * x)
            field[c, pl.ds(pl.multiple_of(2 * FACE + r, BLOCK), BLOCK), :] = x
            split_store(pl.multiple_of(2 * FACE + r, BLOCK), x)
            return norm
        norm = lax.fori_loop(0, NBLK, part, zero8)

        def group(g, curv):
            r = group_row(g)
            value = product(s, r)
            return curv + fold(value * field[c, pl.ds(r, FACE), :])
        curv = lax.fori_loop(0, 3, group, zero8)
        start_sum(c, [row_sum(norm), row_sum(curv)])
        send_up(s)
        send_low(s)
        send_contact(s)
        if c > 0:
            pass_sum(c - 1, 2)

    alphas, norms, curvs, new_norms = [], [], [], []
    for c in range(CHUNKS):
        was, s = CHUNKS + c, 2 * CHUNKS + c
        up_copy(was).wait_recv()
        low_copy(was).wait_recv()
        total_norm, total_curv = end_sum(c, 2)
        alpha = total_norm / total_curv
        alphas.append(alpha)
        norms.append(total_norm)
        curvs.append(total_curv)

        def part(k, carry):
            norm, cross = carry
            r = pl.multiple_of(k * BLOCK, BLOCK)
            for n, of in enumerate((glue_part, upper_part, contact_part)):
                at = pl.multiple_of(n * FACE + r, BLOCK)
                x = field[c, pl.ds(at, BLOCK), :] - alpha * of(was, k)
                if n != 1:
                    norm = norm + fold(x * x)
                cross = cross + fold(x * prod[was, n * NBLK + k])
                first[c, pl.ds(at, BLOCK), :] = x
                split_store(at, x)
            return norm, cross
        norm, cross = lax.fori_loop(0, NBLK, part, (zero8, zero8))

        def group(g, curv):
            r = group_row(g)
            value = product(s, r)
            return curv + fold(value * first[c, pl.ds(r, FACE), :])
        curv = lax.fori_loop(0, 3, group, zero8)
        start_sum(CHUNKS + c, [row_sum(norm), row_sum(cross), row_sum(curv)])
        send_up(s)
        send_contact(s)
        if c == 0:
            pass_sum(CHUNKS - 1, 2)
        else:
            pass_sum(CHUNKS + c - 1, 3)

    for c in range(CHUNKS):
        if c == CHUNKS - 1:
            pass_sum(CHUNKS + c, 3)
        new_norm, cross, curv = end_sum(CHUNKS + c, 3)
        alpha = alphas[c]
        beta = new_norm / norms[c]
        alpha1 = new_norm / (curv + beta * (2.0 * cross + beta * curvs[c]))
        lead = alpha + alpha1 * beta
        for k in range(1, cols):
            con_copy(c, k).wait_recv()
            con_copy(CHUNKS + c, k).wait_recv()
            con_copy(2 * CHUNKS + c, k).wait_recv()

        def contact_out(k, _):
            r = pl.multiple_of(k * BLOCK, BLOCK)
            r0 = con_in[c, k]
            q0 = con_in[CHUNKS + c, k]
            r1 = r0 - alpha * q0
            result[c, 1, pl.ds(r, BLOCK), :] = lead * r0 + alpha1 * r1
            result[c, 3, pl.ds(r, BLOCK), :] = r1 - alpha1 * (con_in[2 * CHUNKS + c, k] + beta * q0)
            return 0
        lax.fori_loop(0, NBLK, contact_out, 0)

        def glue_mult(k, _):
            r = pl.multiple_of(k * BLOCK, BLOCK)
            result[c, 0, pl.ds(r, BLOCK), :] = (
                lead * field[c, pl.ds(r, BLOCK), :] + alpha1 * first[c, pl.ds(r, BLOCK), :])
            return 0
        lax.fori_loop(0, NBLK, glue_mult, 0)

        def out_copy(n, out):
            return pltpu.make_async_copy(result.at[c, n], out.at[:, pl.ds(c * COLS, COLS)], o_sem.at[c, n])
        for n, out in ((0, out_gm), (1, out_cm), (3, out_cr)):
            out_copy(n, out).start()
        up_copy(2 * CHUNKS + c).wait_recv()

        def glue_res(k, _):
            r = pl.multiple_of(k * BLOCK, BLOCK)
            x = glue_part(2 * CHUNKS + c, k) + beta * glue_part(CHUNKS + c, k)
            result[c, 2, pl.ds(r, BLOCK), :] = first[c, pl.ds(r, BLOCK), :] - alpha1 * x
            return 0
        lax.fori_loop(0, NBLK, glue_res, 0)
        out_copy(2, out_gr).start()

    for c in range(CHUNKS):
        for n, out in enumerate((out_gm, out_cm, out_gr, out_cr)):
            pltpu.make_async_copy(result.at[c, n], out.at[:, pl.ds(c * COLS, COLS)], o_sem.at[c, n]).wait()
    for s in range(STEPS):
        up_copy(s).wait_send()
        if s < 2 * CHUNKS:
            low_copy(s).wait_send()
        for k in range(1, cols):
            con_copy(s, k).wait_send()
    for k in range(1, cols):
        flag_copy(k).wait_send()
    for a in range(2 * CHUNKS):
        for k in range(1, rows):
            sub_copy(a, k).wait_send()
        for k in range(1, cols):
            cont_copy(a, k).wait_send()


def hand_on(*refs):
    ins, outs, sem = refs[:4], refs[4:8], refs[8]
    half = FACE // 2
    copies = [
        pltpu.make_async_copy(a.at[pl.ds(h * half, half)], b.at[pl.ds(h * half, half)], sem.at[n, h])
        for n, (a, b) in enumerate(zip(ins, outs)) for h in range(2)
    ]
    for copy in copies:
        copy.start()
    for copy in copies:
        copy.wait()


def per_device(schur_matrix, load_vectors, glue_blocks, contact_order, active_flags):
    rows, cols = lax.axis_size("sub"), lax.axis_size("cont")
    any_space = pl.BlockSpec(memory_space=pl.ANY)
    smem = pl.BlockSpec(memory_space=pltpu.SMEM)
    vmem = pl.BlockSpec(memory_space=pltpu.VMEM)
    dma = pltpu.SemaphoreType.DMA
    sums = 2 * CHUNKS
    outs = pl.pallas_call(
        lambda *refs: kernel(rows, cols, *refs),
        out_shape=[jax.ShapeDtypeStruct((FACE, LOADS), F32)] * 4,
        in_specs=[any_space, any_space, smem, smem, vmem],
        out_specs=[any_space] * 4,
        scratch_shapes=[
            pltpu.VMEM((3, FACE, IFACE), F32),
            pltpu.VMEM((IFACE, IFACE), BF16),
            pltpu.VMEM((IFACE, IFACE), BF16),
            pltpu.VMEM((CHUNKS, IFACE, COLS), F32),
            pltpu.VMEM((IFACE, COLS), BF16),
            pltpu.VMEM((IFACE, COLS), BF16),
            pltpu.VMEM((STEPS, 3 * NBLK, BLOCK, COLS), F32),
            pltpu.VMEM((CHUNKS, IFACE, COLS), F32),
            pltpu.VMEM((NBLK, BLOCK, COLS), F32),
            pltpu.VMEM((2 * CHUNKS, NBLK, BLOCK, COLS), F32),
            pltpu.VMEM((STEPS, NBLK, BLOCK, COLS), F32),
            *[pltpu.VMEM((NBLK, BLOCK, COLS), F32)] * STEPS,
            pltpu.VMEM((2 * CHUNKS, NBLK, BLOCK, COLS), F32),
            pltpu.VMEM((STEPS, NBLK, BLOCK, COLS), F32),
            pltpu.VMEM((cols, 1, FACE), F32),
            pltpu.VMEM((1, FACE), F32),
            pltpu.VMEM((sums, 3, 1, COLS), F32),
            pltpu.VMEM((sums, rows, 3, 1, COLS), F32),
            pltpu.VMEM((sums, 3, 1, COLS), F32),
            pltpu.VMEM((sums, cols, 3, 1, COLS), F32),
            pltpu.VMEM((CHUNKS, 4, FACE, COLS), F32),
            pltpu.SMEM((2, NBLK), jnp.int32),
            dma((3,)), dma((CHUNKS,)), dma((CHUNKS, 4)),
            dma((STEPS,)), dma((STEPS,)),
            dma((2 * CHUNKS,)), dma((2 * CHUNKS,)),
            dma((STEPS, cols)), dma((STEPS, cols)),
            dma((cols,)), dma((cols,)),
            dma((sums, rows)), dma((sums, rows)),
            dma((sums, cols)), dma((sums, cols)),
        ],
        compiler_params=pltpu.CompilerParams(
            collective_id=0, has_side_effects=True, vmem_limit_bytes=60 * 2**20),
        cost_estimate=pl.CostEstimate(
            flops=3 * 6 * IFACE * IFACE * LOADS, bytes_accessed=4 * (IFACE * IFACE + IFACE * LOADS + 4 * FACE * LOADS),
            transcendentals=0),
    )(
        schur_matrix.reshape(IFACE, IFACE),
        load_vectors.reshape(IFACE, LOADS),
        glue_blocks.reshape(1, NBLK),
        contact_order.reshape(1, NBLK),
        active_flags.reshape(1, FACE),
    )
    outs = pl.pallas_call(
        hand_on,
        out_shape=[jax.ShapeDtypeStruct((FACE, LOADS), F32)] * 4,
        in_specs=[any_space] * 4,
        out_specs=[any_space] * 4,
        scratch_shapes=[dma((4, 2))],
    )(*outs)
    return tuple(out[None, None] for out in outs)


def solution(mesh):
    return jax.shard_map(
        per_device,
        mesh=mesh,
        in_specs=(
            P("sub", "cont", None, None),
            P("sub", "cont", None, None),
            P("sub", "cont", None),
            P("sub", "cont", None),
            P("sub", "cont", None),
        ),
        out_specs=(P("sub", "cont", None, None),) * 4,
        check_vma=False,
    )
```

```python
import jax
import jax.numpy as jnp
from jax import lax
from jax.experimental import pallas as pl
from jax.experimental.pallas import tpu as pltpu
from jax.sharding import PartitionSpec as P

BLOCK = 64
NBLK = 8
FACE = BLOCK * NBLK
IFACE = 3 * FACE
LOADS = 512
CHUNKS = 2
COLS = LOADS // CHUNKS
STEPS = 3 * CHUNKS
F32 = jnp.float32
BF16 = jnp.bfloat16


def fold(x):
    return jnp.sum(x.reshape(x.shape[0] // 8, 8, COLS), axis=0)


def row_sum(x):
    return jnp.sum(x, axis=0, keepdims=True)


def kernel(
    rows, cols,
    schur, loads, glue, order, flags,
    out_gm, out_cm, out_gr, out_cr,
    stage_s, s_hi, s_lo, field, f_hi, f_lo, prod, first, mask,
    low_out, con_out, up_in_0, up_in_1, up_in_2, up_in_3, up_in_4, up_in_5, low_in, con_in, flag_in, flag_own,
    sum_own, sum_sub, part_own, sum_con, result, inverse,
    s_sem, l_sem, o_sem,
    up_ss, up_rs, low_ss, low_rs, con_ss, con_rs, flag_ss, flag_rs, sub_ss, sub_rs, cont_ss, cont_rs,
):
    up_in = (up_in_0, up_in_1, up_in_2, up_in_3, up_in_4, up_in_5)
    i = lax.axis_index("sub")
    j = lax.axis_index("cont")
    after = lax.rem(i + 1, rows)
    before = lax.rem(i + rows - 1, rows)
    has_before = i > 0
    has_after = i < rows - 1

    barrier = pltpu.get_barrier_semaphore()
    for k in range(1, rows):
        pl.semaphore_signal(barrier, 1, device_id={"sub": lax.rem(i + k, rows)})
    for k in range(1, cols):
        pl.semaphore_signal(barrier, 1, device_id={"cont": lax.rem(j + k, cols)})

    def load_copy(c):
        return pltpu.make_async_copy(loads.at[:, pl.ds(c * COLS, COLS)], field.at[c], l_sem.at[c])

    def schur_copy(r, slot):
        return pltpu.make_async_copy(schur.at[pl.ds(r, FACE)], stage_s.at[slot], s_sem.at[slot])

    load_copy(0).start()
    schur_copy(FACE, 0).start()
    schur_copy(0, 1).start()
    schur_copy(2 * FACE, 2).start()
    for c in range(1, CHUNKS):
        load_copy(c).start()

    def up_copy(s):
        return pltpu.make_async_remote_copy(
            prod.at[s, pl.ds(NBLK, NBLK)], up_in[s], up_ss.at[s], up_rs.at[s], device_id={"sub": after})

    def low_copy(s):
        return pltpu.make_async_remote_copy(
            low_out.at[s], low_in.at[s], low_ss.at[s], low_rs.at[s], device_id={"sub": before})

    def con_copy(s, k):
        t = lax.rem(j + k, cols)
        return pltpu.make_async_remote_copy(
            con_out.at[s, t], con_in.at[s, j], con_ss.at[s, k], con_rs.at[s, k], device_id={"cont": t})

    def flag_copy(k):
        return pltpu.make_async_remote_copy(
            flag_own, flag_in.at[j], flag_ss.at[k], flag_rs.at[k], device_id={"cont": lax.rem(j + k, cols)})

    def sub_copy(a, k):
        return pltpu.make_async_remote_copy(
            sum_own.at[a], sum_sub.at[a, i], sub_ss.at[a, k], sub_rs.at[a, k], device_id={"sub": lax.rem(i + k, rows)})

    def cont_copy(a, k):
        return pltpu.make_async_remote_copy(
            part_own.at[a], sum_con.at[a, j], cont_ss.at[a, k], cont_rs.at[a, k], device_id={"cont": lax.rem(j + k, cols)})

    for n, ref in enumerate((glue, order)):
        for m in range(NBLK):
            found = jnp.int32(0)
            for k in range(1, NBLK):
                found = jnp.maximum(found, k * (ref[0, k] == m).astype(jnp.int32))
            inverse[n, m] = found

    def split_store(r, x):
        hi = x.astype(BF16)
        f_hi[pl.ds(r, x.shape[0]), :] = hi
        f_lo[pl.ds(r, x.shape[0]), :] = (x - hi.astype(F32)).astype(BF16)

    def product(s, r):
        a_hi = s_hi[pl.ds(r, FACE), :]
        a_lo = s_lo[pl.ds(r, FACE), :]
        value = jnp.dot(a_hi, f_hi[...], preferred_element_type=F32)
        value = value + jnp.dot(a_hi, f_lo[...], preferred_element_type=F32)
        value = value + jnp.dot(a_lo, f_hi[...], preferred_element_type=F32)
        prod[s, pl.ds(lax.div(r, BLOCK), NBLK)] = value.reshape(NBLK, BLOCK, COLS)
        return value

    def group_row(g):
        return pl.multiple_of(jnp.where(g == 0, FACE, jnp.where(g == 1, 0, 2 * FACE)), FACE)

    def send_up(s):
        up_copy(s).start()

    def send_low(s):
        def move(m, _):
            low_out[s, m] = prod[s, inverse[0, m]]
            return 0
        lax.fori_loop(0, NBLK, move, 0)
        low_copy(s).start()

    def send_contact(s):
        def move(t, _):
            con_out[s, t] = prod[s, 2 * NBLK + order[0, t]] * mask[t]
            return 0
        lax.fori_loop(0, NBLK, move, 0)
        for k in range(1, cols):
            con_copy(s, k).start()
        con_in[s, j] = con_out[s, j]

    def glue_part(s, k):
        return prod[s, k] - jnp.where(has_before, up_in[s][glue[0, k]], 0.0)

    def upper_part(s, m):
        return jnp.where(has_after, prod[s, NBLK + m] - low_in[s, m], 0.0)

    def contact_part(s, k):
        return prod[s, 2 * NBLK + k] * mask[inverse[1, k]]

    def start_sum(a, values):
        for n, v in enumerate(values):
            sum_own[a, n] = v
            sum_sub[a, i, n] = v
        for k in range(1, rows):
            sub_copy(a, k).start()

    def pass_sum(a, count):
        for k in range(1, rows):
            sub_copy(a, k).wait_recv()
        for n in range(count):
            v = sum_sub[a, 0, n]
            for k in range(1, rows):
                v = v + sum_sub[a, k, n]
            part_own[a, n] = v
            sum_con[a, j, n] = v
        for k in range(1, cols):
            cont_copy(a, k).start()

    def end_sum(a, count):
        for k in range(1, cols):
            cont_copy(a, k).wait_recv()
        totals = []
        for n in range(count):
            v = sum_con[a, 0, n]
            for k in range(1, cols):
                v = v + sum_con[a, k, n]
            totals.append(v)
        return totals

    zero8 = jnp.zeros((8, COLS), F32)
    zero1 = jnp.zeros((1, COLS), F32)

    for c in range(CHUNKS):
        s = c
        load_copy(c).wait()

        def part(n, _):
            r = pl.multiple_of(n * 128, 128)
            split_store(r, field[c, pl.ds(r, 128), :])
            return 0
        lax.fori_loop(0, IFACE // 128, part, 0)

        def group(g, _):
            r = group_row(g)
            if c == 0:
                schur_copy(r, g).wait()
                x = stage_s[g]
                hi = x.astype(BF16)
                s_hi[pl.ds(r, FACE), :] = hi
                s_lo[pl.ds(r, FACE), :] = (x - hi.astype(F32)).astype(BF16)
            product(s, r)
            if c == 0:
                @pl.when(g == 0)
                def _():
                    pl.semaphore_wait(barrier, rows - 1 + cols - 1)
                    up_copy(0).start()

                @pl.when(g == 1)
                def _():
                    send_low(0)
            return 0
        lax.fori_loop(0, 3, group, 0)
        if c == 0:
            flag_own[...] = flags[...].astype(F32)
            for k in range(1, cols):
                flag_copy(k).start()
            flag_in[j] = flag_own[...]
        else:
            send_up(s)
            send_low(s)

    for k in range(1, cols):
        flag_copy(k).wait_recv()
    lane = lax.broadcasted_iota(jnp.int32, (BLOCK, FACE), 1)
    want = lax.broadcasted_iota(jnp.int32, (BLOCK, FACE), 0) + j * BLOCK

    def mask_of(t, _):
        picked = jnp.where(lane == want, flag_in[t], 0.0)
        mask[t] = jnp.broadcast_to(jnp.sum(picked, axis=1, keepdims=True), (BLOCK, COLS))
        return 0
    lax.fori_loop(0, NBLK, mask_of, 0)

    norms0 = []
    for c in range(CHUNKS):
        was, s = c, CHUNKS + c
        send_contact(was)
        up_copy(was).wait_recv()
        low_copy(was).wait_recv()

        def part(k, norm):
            r = pl.multiple_of(k * BLOCK, BLOCK)
            x = glue_part(was, k)
            norm = norm + fold(x * x)
            field[c, pl.ds(r, BLOCK), :] = x
            split_store(r, x)
            x = upper_part(was, k)
            field[c, pl.ds(pl.multiple_of(FACE + r, BLOCK), BLOCK), :] = x
            split_store(pl.multiple_of(FACE + r, BLOCK), x)
            x = contact_part(was, k)
            norm = norm + fold(x * x)
            field[c, pl.ds(pl.multiple_of(2 * FACE + r, BLOCK), BLOCK), :] = x
            split_store(pl.multiple_of(2 * FACE + r, BLOCK), x)
            return norm
        norm = lax.fori_loop(0, NBLK, part, zero8)

        def group(g, curv):
            r = group_row(g)
            value = product(s, r)
            return curv + fold(value * field[c, pl.ds(r, FACE), :])
        curv = lax.fori_loop(0, 3, group, zero8)
        start_sum(c, [row_sum(norm), row_sum(curv)])
        send_up(s)
        send_low(s)
        send_contact(s)
        if c > 0:
            pass_sum(c - 1, 2)

    alphas, norms, curvs, new_norms = [], [], [], []
    for c in range(CHUNKS):
        was, s = CHUNKS + c, 2 * CHUNKS + c
        up_copy(was).wait_recv()
        low_copy(was).wait_recv()
        total_norm, total_curv = end_sum(c, 2)
        alpha = total_norm / total_curv
        alphas.append(alpha)
        norms.append(total_norm)
        curvs.append(total_curv)

        def part(k, carry):
            norm, cross = carry
            r = pl.multiple_of(k * BLOCK, BLOCK)
            for n, of in enumerate((glue_part, upper_part, contact_part)):
                at = pl.multiple_of(n * FACE + r, BLOCK)
                x = field[c, pl.ds(at, BLOCK), :] - alpha * of(was, k)
                if n != 1:
                    norm = norm + fold(x * x)
                cross = cross + fold(x * prod[was, n * NBLK + k])
                first[c, pl.ds(at, BLOCK), :] = x
                split_store(at, x)
            return norm, cross
        norm, cross = lax.fori_loop(0, NBLK, part, (zero8, zero8))

        def group(g, curv):
            r = group_row(g)
            value = product(s, r)
            return curv + fold(value * first[c, pl.ds(r, FACE), :])
        curv = lax.fori_loop(0, 3, group, zero8)
        start_sum(CHUNKS + c, [row_sum(norm), row_sum(cross), row_sum(curv)])
        send_up(s)
        send_contact(s)
        if c == 0:
            pass_sum(CHUNKS - 1, 2)
        else:
            pass_sum(CHUNKS + c - 1, 3)

    for c in range(CHUNKS):
        if c == CHUNKS - 1:
            pass_sum(CHUNKS + c, 3)
        new_norm, cross, curv = end_sum(CHUNKS + c, 3)
        alpha = alphas[c]
        beta = new_norm / norms[c]
        alpha1 = new_norm / (curv + beta * (2.0 * cross + beta * curvs[c]))
        lead = alpha + alpha1 * beta
        for k in range(1, cols):
            con_copy(c, k).wait_recv()
            con_copy(CHUNKS + c, k).wait_recv()
            con_copy(2 * CHUNKS + c, k).wait_recv()

        def contact_out(k, _):
            r = pl.multiple_of(k * BLOCK, BLOCK)
            r0 = con_in[c, k]
            q0 = con_in[CHUNKS + c, k]
            r1 = r0 - alpha * q0
            result[c, 1, pl.ds(r, BLOCK), :] = lead * r0 + alpha1 * r1
            result[c, 3, pl.ds(r, BLOCK), :] = r1 - alpha1 * (con_in[2 * CHUNKS + c, k] + beta * q0)
            return 0
        lax.fori_loop(0, NBLK, contact_out, 0)

        def glue_mult(k, _):
            r = pl.multiple_of(k * BLOCK, BLOCK)
            result[c, 0, pl.ds(r, BLOCK), :] = (
                lead * field[c, pl.ds(r, BLOCK), :] + alpha1 * first[c, pl.ds(r, BLOCK), :])
            return 0
        lax.fori_loop(0, NBLK, glue_mult, 0)

        def out_copy(n, out):
            return pltpu.make_async_copy(result.at[c, n], out.at[:, pl.ds(c * COLS, COLS)], o_sem.at[c, n])
        for n, out in ((0, out_gm), (1, out_cm), (3, out_cr)):
            out_copy(n, out).start()
        up_copy(2 * CHUNKS + c).wait_recv()

        def glue_res(k, _):
            r = pl.multiple_of(k * BLOCK, BLOCK)
            x = glue_part(2 * CHUNKS + c, k) + beta * glue_part(CHUNKS + c, k)
            result[c, 2, pl.ds(r, BLOCK), :] = first[c, pl.ds(r, BLOCK), :] - alpha1 * x
            return 0
        lax.fori_loop(0, NBLK, glue_res, 0)
        out_copy(2, out_gr).start()

    for c in range(CHUNKS):
        for n, out in enumerate((out_gm, out_cm, out_gr, out_cr)):
            pltpu.make_async_copy(result.at[c, n], out.at[:, pl.ds(c * COLS, COLS)], o_sem.at[c, n]).wait()
    for s in range(STEPS):
        up_copy(s).wait_send()
        if s < 2 * CHUNKS:
            low_copy(s).wait_send()
        for k in range(1, cols):
            con_copy(s, k).wait_send()
    for k in range(1, cols):
        flag_copy(k).wait_send()
    for a in range(2 * CHUNKS):
        for k in range(1, rows):
            sub_copy(a, k).wait_send()
        for k in range(1, cols):
            cont_copy(a, k).wait_send()


def hand_on(*refs):
    ins, outs, held, in_sem, out_sem = refs[:4], refs[4:8], refs[8], refs[9], refs[10]
    half = FACE // 2
    pieces = [(n, h) for n in range(4) for h in range(2)]

    def in_copy(n, h):
        part = pl.ds(h * half, half)
        return pltpu.make_async_copy(ins[n].at[part], held.at[n, part], in_sem.at[n, h])

    def out_copy(n, h):
        part = pl.ds(h * half, half)
        return pltpu.make_async_copy(held.at[n, part], outs[n].at[part], out_sem.at[n, h])

    for n, h in pieces:
        in_copy(n, h).start()
    for n, h in pieces:
        in_copy(n, h).wait()
        out_copy(n, h).start()
    for n, h in pieces:
        out_copy(n, h).wait()


def per_device(schur_matrix, load_vectors, glue_blocks, contact_order, active_flags):
    rows, cols = lax.axis_size("sub"), lax.axis_size("cont")
    any_space = pl.BlockSpec(memory_space=pl.ANY)
    smem = pl.BlockSpec(memory_space=pltpu.SMEM)
    vmem = pl.BlockSpec(memory_space=pltpu.VMEM)
    dma = pltpu.SemaphoreType.DMA
    sums = 2 * CHUNKS
    outs = pl.pallas_call(
        lambda *refs: kernel(rows, cols, *refs),
        out_shape=[jax.ShapeDtypeStruct((FACE, LOADS), F32)] * 4,
        in_specs=[any_space, any_space, smem, smem, vmem],
        out_specs=[any_space] * 4,
        scratch_shapes=[
            pltpu.VMEM((3, FACE, IFACE), F32),
            pltpu.VMEM((IFACE, IFACE), BF16),
            pltpu.VMEM((IFACE, IFACE), BF16),
            pltpu.VMEM((CHUNKS, IFACE, COLS), F32),
            pltpu.VMEM((IFACE, COLS), BF16),
            pltpu.VMEM((IFACE, COLS), BF16),
            pltpu.VMEM((STEPS, 3 * NBLK, BLOCK, COLS), F32),
            pltpu.VMEM((CHUNKS, IFACE, COLS), F32),
            pltpu.VMEM((NBLK, BLOCK, COLS), F32),
            pltpu.VMEM((2 * CHUNKS, NBLK, BLOCK, COLS), F32),
            pltpu.VMEM((STEPS, NBLK, BLOCK, COLS), F32),
            *[pltpu.VMEM((NBLK, BLOCK, COLS), F32)] * STEPS,
            pltpu.VMEM((2 * CHUNKS, NBLK, BLOCK, COLS), F32),
            pltpu.VMEM((STEPS, NBLK, BLOCK, COLS), F32),
            pltpu.VMEM((cols, 1, FACE), F32),
            pltpu.VMEM((1, FACE), F32),
            pltpu.VMEM((sums, 3, 1, COLS), F32),
            pltpu.VMEM((sums, rows, 3, 1, COLS), F32),
            pltpu.VMEM((sums, 3, 1, COLS), F32),
            pltpu.VMEM((sums, cols, 3, 1, COLS), F32),
            pltpu.VMEM((CHUNKS, 4, FACE, COLS), F32),
            pltpu.SMEM((2, NBLK), jnp.int32),
            dma((3,)), dma((CHUNKS,)), dma((CHUNKS, 4)),
            dma((STEPS,)), dma((STEPS,)),
            dma((2 * CHUNKS,)), dma((2 * CHUNKS,)),
            dma((STEPS, cols)), dma((STEPS, cols)),
            dma((cols,)), dma((cols,)),
            dma((sums, rows)), dma((sums, rows)),
            dma((sums, cols)), dma((sums, cols)),
        ],
        compiler_params=pltpu.CompilerParams(
            collective_id=0, has_side_effects=True, vmem_limit_bytes=60 * 2**20),
        cost_estimate=pl.CostEstimate(
            flops=3 * 6 * IFACE * IFACE * LOADS, bytes_accessed=4 * (IFACE * IFACE + IFACE * LOADS + 4 * FACE * LOADS),
            transcendentals=0),
    )(
        schur_matrix.reshape(IFACE, IFACE),
        load_vectors.reshape(IFACE, LOADS),
        glue_blocks.reshape(1, NBLK),
        contact_order.reshape(1, NBLK),
        active_flags.reshape(1, FACE),
    )
    outs = pl.pallas_call(
        hand_on,
        out_shape=[jax.ShapeDtypeStruct((FACE, LOADS), F32)] * 4,
        in_specs=[any_space] * 4,
        out_specs=[any_space] * 4,
        scratch_shapes=[pltpu.VMEM((4, FACE, LOADS), F32), dma((4, 2)), dma((4, 2))],
    )(*outs)
    return tuple(out[None, None] for out in outs)


def solution(mesh):
    return jax.shard_map(
        per_device,
        mesh=mesh,
        in_specs=(
            P("sub", "cont", None, None),
            P("sub", "cont", None, None),
            P("sub", "cont", None),
            P("sub", "cont", None),
            P("sub", "cont", None),
        ),
        out_specs=(P("sub", "cont", None, None),) * 4,
        check_vma=False,
    )
```

```python
import jax
import jax.numpy as jnp
from jax import lax
from jax.experimental import pallas as pl
from jax.experimental.pallas import tpu as pltpu
from jax.sharding import PartitionSpec as P

BLOCK = 64
NBLK = 8
HALF = NBLK // 2
FACE = BLOCK * NBLK
IFACE = 3 * FACE
LOADS = 512
CHUNKS = 2
COLS = LOADS // CHUNKS
PIECES = 6
PIECE = IFACE // PIECES
STEPS = 3 * CHUNKS
F32 = jnp.float32
BF16 = jnp.bfloat16


def fold(x):
    return jnp.sum(x.reshape(x.shape[0] // 8, 8, COLS), axis=0)


def row_sum(x):
    return jnp.sum(x, axis=0, keepdims=True)


def kernel(
    rows, cols,
    schur, loads, glue_hbm, order_hbm, flags_hbm,
    out_gm, out_cm, out_gr, out_cr,
    stage_s, s_hi, s_lo, field, f_hi, f_lo, prod, first, mask,
    low_out, con_out, up_in_0, up_in_1, up_in_2, up_in_3, up_in_4, up_in_5, low_in, con_in, flag_in, flag_own,
    sum_own, sum_sub, part_own, sum_con, inverse, glue, order, flags,
    s_sem, l_sem, i_sem,
    half_ss, half_rs, up_ss, up_rs, low_ss, low_rs, con_ss, con_rs, flag_ss, flag_rs, sub_ss, sub_rs, cont_ss, cont_rs,
):
    up_in = (up_in_0, up_in_1, up_in_2, up_in_3, up_in_4, up_in_5)
    i = lax.axis_index("sub")
    j = lax.axis_index("cont")
    after = lax.rem(i + 1, rows)
    before = lax.rem(i + rows - 1, rows)
    has_before = i > 0
    has_after = i < rows - 1

    barrier = pltpu.get_barrier_semaphore()
    for k in range(1, rows):
        pl.semaphore_signal(barrier, 1, device_id={"sub": lax.rem(i + k, rows)})
    for k in range(1, cols):
        pl.semaphore_signal(barrier, 1, device_id={"cont": lax.rem(j + k, cols)})

    def load_copy(c):
        return pltpu.make_async_copy(loads.at[:, pl.ds(c * COLS, COLS)], field.at[c], l_sem.at[c])

    def piece_row(g):
        n = jnp.where(g == 0, 2, jnp.where(g < 3, g - 1, g))
        return pl.multiple_of(n * PIECE, PIECE)

    def schur_copy(g):
        return pltpu.make_async_copy(schur.at[pl.ds(piece_row(g), PIECE)], stage_s.at[g], s_sem.at[g])

    small_copies = [
        pltpu.make_async_copy(a, b, i_sem.at[n])
        for n, (a, b) in enumerate(((glue_hbm, glue), (order_hbm, order), (flags_hbm, flags)))
    ]
    load_copy(0).start()
    schur_copy(0).start()
    for copy in small_copies:
        copy.start()
    schur_copy(1).start()

    def first_up_copy(h):
        part = pl.ds(NBLK + h * HALF, HALF)
        return pltpu.make_async_remote_copy(
            prod.at[0, part], up_in[0].at[pl.ds(h * HALF, HALF)], half_ss.at[h], half_rs.at[h], device_id={"sub": after})

    def up_copy(s):
        return pltpu.make_async_remote_copy(
            prod.at[s, pl.ds(NBLK, NBLK)], up_in[s], up_ss.at[s], up_rs.at[s], device_id={"sub": after})

    def low_copy(s):
        return pltpu.make_async_remote_copy(
            low_out.at[s], low_in.at[s], low_ss.at[s], low_rs.at[s], device_id={"sub": before})

    def con_copy(s, k):
        t = lax.rem(j + k, cols)
        return pltpu.make_async_remote_copy(
            con_out.at[s, t], con_in.at[s, j], con_ss.at[s, k], con_rs.at[s, k], device_id={"cont": t})

    def flag_copy(k):
        return pltpu.make_async_remote_copy(
            flag_own, flag_in.at[j], flag_ss.at[k], flag_rs.at[k], device_id={"cont": lax.rem(j + k, cols)})

    def held(a):
        return pl.ds(0, 2 if a < CHUNKS else 3)

    def sub_copy(a, k):
        return pltpu.make_async_remote_copy(
            sum_own.at[a, held(a)], sum_sub.at[a, i, held(a)], sub_ss.at[a, k], sub_rs.at[a, k], device_id={"sub": lax.rem(i + k, rows)})

    def cont_copy(a, k):
        return pltpu.make_async_remote_copy(
            part_own.at[a, held(a)], sum_con.at[a, j, held(a)], cont_ss.at[a, k], cont_rs.at[a, k], device_id={"cont": lax.rem(j + k, cols)})

    def make_inverse():
        for n, ref in enumerate((glue, order)):
            for m in range(NBLK):
                found = jnp.int32(0)
                for k in range(1, NBLK):
                    found = jnp.maximum(found, k * (ref[0, k] == m).astype(jnp.int32))
                inverse[n, m] = found

    def split_store(r, x):
        hi = x.astype(BF16)
        f_hi[pl.ds(r, x.shape[0]), :] = hi
        f_lo[pl.ds(r, x.shape[0]), :] = (x - hi.astype(F32)).astype(BF16)

    def product(s, r, size=FACE):
        a_hi = s_hi[pl.ds(r, size), :]
        a_lo = s_lo[pl.ds(r, size), :]
        value = jnp.dot(a_hi, f_hi[...], preferred_element_type=F32)
        value = value + jnp.dot(a_hi, f_lo[...], preferred_element_type=F32)
        value = value + jnp.dot(a_lo, f_hi[...], preferred_element_type=F32)
        prod[s, pl.ds(lax.div(r, BLOCK), size // BLOCK)] = value.reshape(size // BLOCK, BLOCK, COLS)
        return value

    def group_row(g):
        return pl.multiple_of(jnp.where(g == 0, FACE, jnp.where(g == 1, 0, 2 * FACE)), FACE)

    def send_up(s):
        up_copy(s).start()

    def send_low(s):
        def move(m, _):
            low_out[s, m] = prod[s, inverse[0, m]]
            return 0
        lax.fori_loop(0, NBLK, move, 0)
        low_copy(s).start()

    def send_contact(s):
        def move(t, _):
            con_out[s, t] = prod[s, 2 * NBLK + order[0, t]] * mask[t]
            return 0
        lax.fori_loop(0, NBLK, move, 0)
        for k in range(1, cols):
            con_copy(s, k).start()
        con_in[s, j] = con_out[s, j]

    def glue_part(s, k):
        return prod[s, k] - jnp.where(has_before, up_in[s][glue[0, k]], 0.0)

    def upper_part(s, m):
        return jnp.where(has_after, prod[s, NBLK + m] - low_in[s, m], 0.0)

    def contact_part(s, k):
        return prod[s, 2 * NBLK + k] * mask[inverse[1, k]]

    def start_sum(a, values):
        for n, v in enumerate(values):
            sum_own[a, n] = v
            sum_sub[a, i, n] = v
        for k in range(1, rows):
            sub_copy(a, k).start()

    def pass_sum(a, count):
        for k in range(1, rows):
            sub_copy(a, k).wait_recv()
        for n in range(count):
            v = sum_sub[a, 0, n]
            for k in range(1, rows):
                v = v + sum_sub[a, k, n]
            part_own[a, n] = v
            sum_con[a, j, n] = v
        for k in range(1, cols):
            cont_copy(a, k).start()

    def end_sum(a, count):
        for k in range(1, cols):
            cont_copy(a, k).wait_recv()
        totals = []
        for n in range(count):
            v = sum_con[a, 0, n]
            for k in range(1, cols):
                v = v + sum_con[a, k, n]
            totals.append(v)
        return totals

    zero8 = jnp.zeros((8, COLS), F32)
    zero1 = jnp.zeros((1, COLS), F32)

    def split_loads(c):
        def part(n, _):
            r = pl.multiple_of(n * 128, 128)
            split_store(r, field[c, pl.ds(r, 128), :])
            return 0
        lax.fori_loop(0, IFACE // 128, part, 0)

    load_copy(0).wait()
    schur_copy(2).start()
    split_loads(0)

    def piece(g, _):
        r = piece_row(g)
        schur_copy(g).wait()

        @pl.when(g < PIECES - 3)
        def _():
            schur_copy(g + 3).start()
        x = stage_s[g]
        hi = x.astype(BF16)
        s_hi[pl.ds(r, PIECE), :] = hi
        s_lo[pl.ds(r, PIECE), :] = (x - hi.astype(F32)).astype(BF16)
        product(0, r, PIECE)

        @pl.when(g == 0)
        def _():
            pl.semaphore_wait(barrier, rows - 1 + cols - 1)
            first_up_copy(0).start()
            for copy in small_copies:
                copy.wait()
            make_inverse()

        @pl.when(g == 2)
        def _():
            send_low(0)

        @pl.when(g == 3)
        def _():
            first_up_copy(1).start()
            for c in range(1, CHUNKS):
                load_copy(c).start()
        return 0
    lax.fori_loop(0, PIECES, piece, 0)
    flag_own[...] = flags[...].astype(F32)
    for k in range(1, cols):
        flag_copy(k).start()
    flag_in[j] = flag_own[...]

    for c in range(1, CHUNKS):
        load_copy(c).wait()
        split_loads(c)

        def group(g, _):
            product(c, group_row(g))
            return 0
        lax.fori_loop(0, 3, group, 0)
        send_up(c)
        send_low(c)

    for k in range(1, cols):
        flag_copy(k).wait_recv()
    lane = lax.broadcasted_iota(jnp.int32, (BLOCK, FACE), 1)
    want = lax.broadcasted_iota(jnp.int32, (BLOCK, FACE), 0) + j * BLOCK

    def mask_of(t, _):
        picked = jnp.where(lane == want, flag_in[t], 0.0)
        mask[t] = jnp.broadcast_to(jnp.sum(picked, axis=1, keepdims=True), (BLOCK, COLS))
        return 0
    lax.fori_loop(0, NBLK, mask_of, 0)

    norms0 = []
    for c in range(CHUNKS):
        was, s = c, CHUNKS + c
        send_contact(was)
        if c == 0:
            first_up_copy(0).wait_recv()
            first_up_copy(1).wait_recv()
        else:
            up_copy(was).wait_recv()
        low_copy(was).wait_recv()

        def part(k, norm):
            r = pl.multiple_of(k * BLOCK, BLOCK)
            x = glue_part(was, k)
            norm = norm + fold(x * x)
            field[c, pl.ds(r, BLOCK), :] = x
            split_store(r, x)
            x = upper_part(was, k)
            field[c, pl.ds(pl.multiple_of(FACE + r, BLOCK), BLOCK), :] = x
            split_store(pl.multiple_of(FACE + r, BLOCK), x)
            x = contact_part(was, k)
            norm = norm + fold(x * x)
            field[c, pl.ds(pl.multiple_of(2 * FACE + r, BLOCK), BLOCK), :] = x
            split_store(pl.multiple_of(2 * FACE + r, BLOCK), x)
            return norm
        norm = lax.fori_loop(0, NBLK, part, zero8)

        def group(g, curv):
            r = group_row(g)
            value = product(s, r)
            return curv + fold(value * field[c, pl.ds(r, FACE), :])
        curv = lax.fori_loop(0, 3, group, zero8)
        start_sum(c, [row_sum(norm), row_sum(curv)])
        send_up(s)
        send_low(s)
        send_contact(s)
        if c > 0:
            pass_sum(c - 1, 2)

    alphas, norms, curvs, new_norms = [], [], [], []
    for c in range(CHUNKS):
        was, s = CHUNKS + c, 2 * CHUNKS + c
        up_copy(was).wait_recv()
        low_copy(was).wait_recv()
        total_norm, total_curv = end_sum(c, 2)
        alpha = total_norm / total_curv
        alphas.append(alpha)
        norms.append(total_norm)
        curvs.append(total_curv)

        def part(k, carry):
            norm, cross = carry
            r = pl.multiple_of(k * BLOCK, BLOCK)
            for n, of in enumerate((glue_part, upper_part, contact_part)):
                at = pl.multiple_of(n * FACE + r, BLOCK)
                x = field[c, pl.ds(at, BLOCK), :] - alpha * of(was, k)
                if n != 1:
                    norm = norm + fold(x * x)
                cross = cross + fold(x * prod[was, n * NBLK + k])
                first[c, pl.ds(at, BLOCK), :] = x
                split_store(at, x)
            return norm, cross
        norm, cross = lax.fori_loop(0, NBLK, part, (zero8, zero8))

        def group(g, curv):
            r = group_row(g)
            value = product(s, r)
            return curv + fold(value * first[c, pl.ds(r, FACE), :])
        curv = lax.fori_loop(0, 3, group, zero8)
        start_sum(CHUNKS + c, [row_sum(norm), row_sum(cross), row_sum(curv)])
        send_up(s)
        send_contact(s)
        if c == 0:
            pass_sum(CHUNKS - 1, 2)
        else:
            pass_sum(CHUNKS + c - 1, 3)

    for c in range(CHUNKS):
        if c == CHUNKS - 1:
            pass_sum(CHUNKS + c, 3)
        new_norm, cross, curv = end_sum(CHUNKS + c, 3)
        alpha = alphas[c]
        beta = new_norm / norms[c]
        alpha1 = new_norm / (curv + beta * (2.0 * cross + beta * curvs[c]))
        lead = alpha + alpha1 * beta
        for k in range(1, cols):
            con_copy(c, k).wait_recv()
            con_copy(CHUNKS + c, k).wait_recv()
            con_copy(2 * CHUNKS + c, k).wait_recv()

        def contact_out(k, _):
            r = pl.multiple_of(k * BLOCK, BLOCK)
            r0 = con_in[c, k]
            q0 = con_in[CHUNKS + c, k]
            r1 = r0 - alpha * q0
            out_cm[pl.ds(r, BLOCK), pl.ds(c * COLS, COLS)] = lead * r0 + alpha1 * r1
            out_cr[pl.ds(r, BLOCK), pl.ds(c * COLS, COLS)] = r1 - alpha1 * (con_in[2 * CHUNKS + c, k] + beta * q0)
            return 0
        lax.fori_loop(0, NBLK, contact_out, 0)

        def glue_mult(k, _):
            r = pl.multiple_of(k * BLOCK, BLOCK)
            out_gm[pl.ds(r, BLOCK), pl.ds(c * COLS, COLS)] = (
                lead * field[c, pl.ds(r, BLOCK), :] + alpha1 * first[c, pl.ds(r, BLOCK), :])
            return 0
        lax.fori_loop(0, NBLK, glue_mult, 0)

        up_copy(2 * CHUNKS + c).wait_recv()

        def glue_res(k, _):
            r = pl.multiple_of(k * BLOCK, BLOCK)
            x = glue_part(2 * CHUNKS + c, k) + beta * glue_part(CHUNKS + c, k)
            out_gr[pl.ds(r, BLOCK), pl.ds(c * COLS, COLS)] = first[c, pl.ds(r, BLOCK), :] - alpha1 * x
            return 0
        lax.fori_loop(0, NBLK, glue_res, 0)

    for s in range(STEPS):
        if s > 0:
            up_copy(s).wait_send()
        if s < 2 * CHUNKS:
            low_copy(s).wait_send()
        for k in range(1, cols):
            con_copy(s, k).wait_send()
    first_up_copy(0).wait_send()
    first_up_copy(1).wait_send()
    for k in range(1, cols):
        flag_copy(k).wait_send()
    for a in range(2 * CHUNKS):
        for k in range(1, rows):
            sub_copy(a, k).wait_send()
        for k in range(1, cols):
            cont_copy(a, k).wait_send()


def hand_on(*refs):
    ins, outs, sem = refs[:4], refs[4:8], refs[8]
    copies = [pltpu.make_async_copy(a, b, sem.at[n]) for n, (a, b) in enumerate(zip(ins, outs))]
    for copy in copies:
        copy.start()
    for copy in copies:
        copy.wait()


def per_device(schur_matrix, load_vectors, glue_blocks, contact_order, active_flags):
    rows, cols = lax.axis_size("sub"), lax.axis_size("cont")
    any_space = pl.BlockSpec(memory_space=pl.ANY)
    vmem = pl.BlockSpec(memory_space=pltpu.VMEM)
    dma = pltpu.SemaphoreType.DMA
    sums = 2 * CHUNKS
    outs = pl.pallas_call(
        lambda *refs: kernel(rows, cols, *refs),
        out_shape=[pltpu.VMEM((FACE, LOADS), F32)] * 4,
        in_specs=[any_space] * 5,
        out_specs=[vmem] * 4,
        scratch_shapes=[
            pltpu.VMEM((PIECES, PIECE, IFACE), F32),
            pltpu.VMEM((IFACE, IFACE), BF16),
            pltpu.VMEM((IFACE, IFACE), BF16),
            pltpu.VMEM((CHUNKS, IFACE, COLS), F32),
            pltpu.VMEM((IFACE, COLS), BF16),
            pltpu.VMEM((IFACE, COLS), BF16),
            pltpu.VMEM((STEPS, 3 * NBLK, BLOCK, COLS), F32),
            pltpu.VMEM((CHUNKS, IFACE, COLS), F32),
            pltpu.VMEM((NBLK, BLOCK, COLS), F32),
            pltpu.VMEM((2 * CHUNKS, NBLK, BLOCK, COLS), F32),
            pltpu.VMEM((STEPS, NBLK, BLOCK, COLS), F32),
            *[pltpu.VMEM((NBLK, BLOCK, COLS), F32)] * STEPS,
            pltpu.VMEM((2 * CHUNKS, NBLK, BLOCK, COLS), F32),
            pltpu.VMEM((STEPS, NBLK, BLOCK, COLS), F32),
            pltpu.VMEM((cols, 1, FACE), F32),
            pltpu.VMEM((1, FACE), F32),
            pltpu.VMEM((sums, 3, 1, COLS), F32),
            pltpu.VMEM((sums, rows, 3, 1, COLS), F32),
            pltpu.VMEM((sums, 3, 1, COLS), F32),
            pltpu.VMEM((sums, cols, 3, 1, COLS), F32),
            pltpu.SMEM((2, NBLK), jnp.int32),
            pltpu.SMEM((1, NBLK), jnp.int32),
            pltpu.SMEM((1, NBLK), jnp.int32),
            pltpu.VMEM((1, FACE), jnp.int32),
            dma((PIECES,)), dma((CHUNKS,)), dma((3,)),
            dma((2,)), dma((2,)), dma((STEPS,)), dma((STEPS,)),
            dma((2 * CHUNKS,)), dma((2 * CHUNKS,)),
            dma((STEPS, cols)), dma((STEPS, cols)),
            dma((cols,)), dma((cols,)),
            dma((sums, rows)), dma((sums, rows)),
            dma((sums, cols)), dma((sums, cols)),
        ],
        compiler_params=pltpu.CompilerParams(
            collective_id=0, has_side_effects=True, vmem_limit_bytes=54 * 2**20),
        cost_estimate=pl.CostEstimate(
            flops=3 * 6 * IFACE * IFACE * LOADS, bytes_accessed=4 * (IFACE * IFACE + IFACE * LOADS + 4 * FACE * LOADS),
            transcendentals=0),
    )(
        schur_matrix.reshape(IFACE, IFACE),
        load_vectors.reshape(IFACE, LOADS),
        glue_blocks.reshape(1, NBLK),
        contact_order.reshape(1, NBLK),
        active_flags.reshape(1, FACE),
    )
    outs = pl.pallas_call(
        hand_on,
        out_shape=[jax.ShapeDtypeStruct((FACE, LOADS), F32)] * 4,
        in_specs=[vmem] * 4,
        out_specs=[any_space] * 4,
        scratch_shapes=[dma((4,))],
        compiler_params=pltpu.CompilerParams(vmem_limit_bytes=4 * 2**20),
    )(*outs)
    return tuple(out[None, None] for out in outs)


def solution(mesh):
    return jax.shard_map(
        per_device,
        mesh=mesh,
        in_specs=(
            P("sub", "cont", None, None),
            P("sub", "cont", None, None),
            P("sub", "cont", None),
            P("sub", "cont", None),
            P("sub", "cont", None),
        ),
        out_specs=(P("sub", "cont", None, None),) * 4,
        check_vma=False,
    )
```

```python
import jax
import jax.numpy as jnp
from jax import lax
from jax.experimental import pallas as pl
from jax.experimental.pallas import tpu as pltpu
from jax.sharding import PartitionSpec as P

BLOCK = 64
NBLK = 8
HALF = NBLK // 2
ROUND = 3
RING = 4
FACE = BLOCK * NBLK
IFACE = 3 * FACE
LOADS = 512
CHUNKS = 2
COLS = LOADS // CHUNKS
PIECES = 6
PIECE = IFACE // PIECES
STEPS = 3 * CHUNKS
F32 = jnp.float32
BF16 = jnp.bfloat16


def fold(x):
    return jnp.sum(x.reshape(x.shape[0] // 8, 8, COLS), axis=0)


def row_sum(x):
    return jnp.sum(x, axis=0, keepdims=True)


def kernel(
    rows, cols,
    schur, loads, glue_hbm, order_hbm, flags_hbm,
    out_gm, out_cm, out_gr, out_cr,
    stage_s, s_hi, s_lo, field, f_hi, f_lo, prod, first, mask,
    low_out, con_out, up_in_0, up_in_1, up_in_2, up_in_3, up_in_4, up_in_5, low_in, con_in, flag_in, flag_own,
    sum_own, sum_sub, part_own, sum_con, inverse, glue, order, flags, relay_1, relay_2,
    s_sem, l_sem, i_sem,
    last_ss, last_rs, hop_ss, hop_rs, half_ss, half_rs, up_ss, up_rs, low_ss, low_rs, con_ss, con_rs, flag_ss, flag_rs, sub_ss, sub_rs, cont_ss, cont_rs,
):
    up_in = (up_in_0, up_in_1, up_in_2, up_in_3, up_in_4, up_in_5)
    i = lax.axis_index("sub")
    j = lax.axis_index("cont")
    after = lax.rem(i + 1, rows)
    before = lax.rem(i + rows - 1, rows)
    has_before = i > 0
    has_after = i < rows - 1

    barrier = pltpu.get_barrier_semaphore()
    for k in range(1, rows):
        pl.semaphore_signal(barrier, 1, device_id={"sub": lax.rem(i + k, rows)})
    for k in range(1, cols):
        pl.semaphore_signal(barrier, 1, device_id={"cont": lax.rem(j + k, cols)})

    def load_copy(c):
        return pltpu.make_async_copy(loads.at[:, pl.ds(c * COLS, COLS)], field.at[c], l_sem.at[c])

    def piece_row(g):
        n = jnp.where(g == 0, 2, jnp.where(g < 3, g - 1, g))
        return pl.multiple_of(n * PIECE, PIECE)

    def schur_copy(g):
        return pltpu.make_async_copy(schur.at[pl.ds(piece_row(g), PIECE)], stage_s.at[g], s_sem.at[g])

    small_copies = [
        pltpu.make_async_copy(a, b, i_sem.at[n])
        for n, (a, b) in enumerate(((glue_hbm, glue), (order_hbm, order), (flags_hbm, flags)))
    ]
    load_copy(0).start()
    schur_copy(0).start()
    for copy in small_copies:
        copy.start()
    schur_copy(1).start()

    def first_up_copy(h):
        part = pl.ds(NBLK + h * HALF, HALF)
        return pltpu.make_async_remote_copy(
            prod.at[0, part], up_in[0].at[pl.ds(h * HALF, HALF)], half_ss.at[h], half_rs.at[h], device_id={"sub": after})

    def last_up_copy(h):
        s = STEPS - 1
        return pltpu.make_async_remote_copy(
            prod.at[s, pl.ds(NBLK + h * HALF, HALF)], up_in[s].at[pl.ds(h * HALF, HALF)], last_ss.at[h], last_rs.at[h],
            device_id={"sub": after})

    def up_copy(s):
        count = NBLK - ROUND if s == 2 * CHUNKS else NBLK
        return pltpu.make_async_remote_copy(
            prod.at[s, pl.ds(NBLK, count)], up_in[s].at[pl.ds(0, count)], up_ss.at[s], up_rs.at[s],
            device_id={"sub": after})

    ring = lax.rem(i, RING)
    ring_down = i - ring + lax.rem(ring + RING - 1, RING)
    two_down_after = lax.rem(i - ring + lax.rem(ring + 2, RING) + 1, rows)

    def hop_copy(n):
        s = 2 * CHUNKS
        kept = pl.ds(NBLK - ROUND, ROUND)
        src = (prod.at[s, pl.ds(2 * NBLK - ROUND, ROUND)], relay_1, relay_2)[n]
        dst = (relay_1, relay_2, up_in[s].at[kept])[n]
        to = (ring_down, ring_down, two_down_after)[n]
        return pltpu.make_async_remote_copy(src, dst, hop_ss.at[n], hop_rs.at[n], device_id={"sub": to})

    def low_copy(s):
        return pltpu.make_async_remote_copy(
            low_out.at[s], low_in.at[s], low_ss.at[s], low_rs.at[s], device_id={"sub": before})

    def con_copy(s, k):
        t = lax.rem(j + k, cols)
        return pltpu.make_async_remote_copy(
            con_out.at[s, t], con_in.at[s, j], con_ss.at[s, k], con_rs.at[s, k], device_id={"cont": t})

    def flag_copy(k):
        return pltpu.make_async_remote_copy(
            flag_own, flag_in.at[j], flag_ss.at[k], flag_rs.at[k], device_id={"cont": lax.rem(j + k, cols)})

    def held(a):
        return pl.ds(0, 2 if a < CHUNKS else 3)

    def sub_copy(a, k):
        return pltpu.make_async_remote_copy(
            sum_own.at[a, held(a)], sum_sub.at[a, i, held(a)], sub_ss.at[a, k], sub_rs.at[a, k], device_id={"sub": lax.rem(i + k, rows)})

    def cont_copy(a, k):
        return pltpu.make_async_remote_copy(
            part_own.at[a, held(a)], sum_con.at[a, j, held(a)], cont_ss.at[a, k], cont_rs.at[a, k], device_id={"cont": lax.rem(j + k, cols)})

    def make_inverse():
        for n, ref in enumerate((glue, order)):
            for m in range(NBLK):
                found = jnp.int32(0)
                for k in range(1, NBLK):
                    found = jnp.maximum(found, k * (ref[0, k] == m).astype(jnp.int32))
                inverse[n, m] = found

    def split_store(r, x):
        hi = x.astype(BF16)
        f_hi[pl.ds(r, x.shape[0]), :] = hi
        f_lo[pl.ds(r, x.shape[0]), :] = (x - hi.astype(F32)).astype(BF16)

    def product(s, r, size=FACE):
        a_hi = s_hi[pl.ds(r, size), :]
        a_lo = s_lo[pl.ds(r, size), :]
        value = jnp.dot(a_hi, f_hi[...], preferred_element_type=F32)
        value = value + jnp.dot(a_hi, f_lo[...], preferred_element_type=F32)
        value = value + jnp.dot(a_lo, f_hi[...], preferred_element_type=F32)
        prod[s, pl.ds(lax.div(r, BLOCK), size // BLOCK)] = value.reshape(size // BLOCK, BLOCK, COLS)
        return value

    def group_row(g):
        return pl.multiple_of(jnp.where(g == 0, FACE, jnp.where(g == 1, 0, 2 * FACE)), FACE)

    def product_row(g):
        return pl.multiple_of((2 - g) * FACE, FACE)

    def send_up(s):
        up_copy(s).start()

    def send_low(s):
        def move(m, _):
            low_out[s, m] = prod[s, inverse[0, m]]
            return 0
        lax.fori_loop(0, NBLK, move, 0)
        low_copy(s).start()

    def send_contact(s):
        def move(t, _):
            con_out[s, t] = prod[s, 2 * NBLK + order[0, t]] * mask[t]
            return 0
        lax.fori_loop(0, NBLK, move, 0)
        for k in range(1, cols):
            con_copy(s, k).start()
        con_in[s, j] = con_out[s, j]

    def glue_part(s, k):
        return prod[s, k] - jnp.where(has_before, up_in[s][glue[0, k]], 0.0)

    def upper_part(s, m):
        return jnp.where(has_after, prod[s, NBLK + m] - low_in[s, m], 0.0)

    def contact_part(s, k):
        return prod[s, 2 * NBLK + k] * mask[inverse[1, k]]

    def start_sum(a, values):
        for n, v in enumerate(values):
            sum_own[a, n] = v
            sum_sub[a, i, n] = v
        for k in range(1, rows):
            sub_copy(a, k).start()

    def pass_sum(a, count):
        for k in range(1, rows):
            sub_copy(a, k).wait_recv()
        for n in range(count):
            v = sum_sub[a, 0, n]
            for k in range(1, rows):
                v = v + sum_sub[a, k, n]
            part_own[a, n] = v
            sum_con[a, j, n] = v
        for k in range(1, cols):
            cont_copy(a, k).start()

    def end_sum(a, count):
        for k in range(1, cols):
            cont_copy(a, k).wait_recv()
        totals = []
        for n in range(count):
            v = sum_con[a, 0, n]
            for k in range(1, cols):
                v = v + sum_con[a, k, n]
            totals.append(v)
        return totals

    zero8 = jnp.zeros((8, COLS), F32)
    zero1 = jnp.zeros((1, COLS), F32)

    def split_loads(c):
        def part(n, _):
            r = pl.multiple_of(n * 128, 128)
            split_store(r, field[c, pl.ds(r, 128), :])
            return 0
        lax.fori_loop(0, IFACE // 128, part, 0)

    load_copy(0).wait()
    schur_copy(2).start()
    split_loads(0)

    def piece(g, _):
        r = piece_row(g)
        schur_copy(g).wait()

        @pl.when(g < PIECES - 3)
        def _():
            schur_copy(g + 3).start()
        x = stage_s[g]
        hi = x.astype(BF16)
        s_hi[pl.ds(r, PIECE), :] = hi
        s_lo[pl.ds(r, PIECE), :] = (x - hi.astype(F32)).astype(BF16)
        product(0, r, PIECE)

        @pl.when(g == 0)
        def _():
            pl.semaphore_wait(barrier, rows - 1 + cols - 1)
            first_up_copy(0).start()
            for copy in small_copies:
                copy.wait()
            make_inverse()

        @pl.when(g == 2)
        def _():
            send_low(0)

        @pl.when(g == 3)
        def _():
            first_up_copy(1).start()
            for c in range(1, CHUNKS):
                load_copy(c).start()
        return 0
    lax.fori_loop(0, PIECES, piece, 0)
    flag_own[...] = flags[...].astype(F32)
    for k in range(1, cols):
        flag_copy(k).start()
    flag_in[j] = flag_own[...]

    for c in range(1, CHUNKS):
        load_copy(c).wait()
        split_loads(c)

        def group(g, _):
            product(c, group_row(g))
            return 0
        lax.fori_loop(0, 3, group, 0)
        send_up(c)
        send_low(c)

    for k in range(1, cols):
        flag_copy(k).wait_recv()
    lane = lax.broadcasted_iota(jnp.int32, (BLOCK, FACE), 1)
    want = lax.broadcasted_iota(jnp.int32, (BLOCK, FACE), 0) + j * BLOCK

    def mask_of(t, _):
        picked = jnp.where(lane == want, flag_in[t], 0.0)
        mask[t] = jnp.broadcast_to(jnp.sum(picked, axis=1, keepdims=True), (BLOCK, COLS))
        return 0
    lax.fori_loop(0, NBLK, mask_of, 0)

    for c in range(CHUNKS):
        send_contact(c)

    for c in range(CHUNKS):
        was, s = c, CHUNKS + c
        if c == 0:
            first_up_copy(0).wait_recv()
            first_up_copy(1).wait_recv()
        else:
            up_copy(was).wait_recv()
        low_copy(was).wait_recv()

        def part(k, norm):
            r = pl.multiple_of(k * BLOCK, BLOCK)
            x = glue_part(was, k)
            norm = norm + fold(x * x)
            field[c, pl.ds(r, BLOCK), :] = x
            split_store(r, x)
            x = upper_part(was, k)
            field[c, pl.ds(pl.multiple_of(FACE + r, BLOCK), BLOCK), :] = x
            split_store(pl.multiple_of(FACE + r, BLOCK), x)
            x = contact_part(was, k)
            norm = norm + fold(x * x)
            field[c, pl.ds(pl.multiple_of(2 * FACE + r, BLOCK), BLOCK), :] = x
            split_store(pl.multiple_of(2 * FACE + r, BLOCK), x)
            return norm
        norm = lax.fori_loop(0, NBLK, part, zero8)

        if c > 0:
            pass_sum(c - 1, 2)

        def group(g, curv):
            r = product_row(g)
            value = product(s, r)

            @pl.when(g == 0)
            def _():
                send_contact(s)
            return curv + fold(value * field[c, pl.ds(r, FACE), :])
        curv = lax.fori_loop(0, 3, group, zero8)
        start_sum(c, [row_sum(norm), row_sum(curv)])
        send_up(s)
        send_low(s)

    alphas, norms, curvs = [], [], []
    for c in range(CHUNKS):
        was, s = CHUNKS + c, 2 * CHUNKS + c
        up_copy(was).wait_recv()
        low_copy(was).wait_recv()
        total_norm, total_curv = end_sum(c, 2)
        alpha = total_norm / total_curv
        alphas.append(alpha)
        norms.append(total_norm)
        curvs.append(total_curv)

        def part(k, carry):
            norm, cross = carry
            r = pl.multiple_of(k * BLOCK, BLOCK)
            for n, of in enumerate((glue_part, upper_part, contact_part)):
                at = pl.multiple_of(n * FACE + r, BLOCK)
                x = field[c, pl.ds(at, BLOCK), :] - alpha * of(was, k)
                if n != 1:
                    norm = norm + fold(x * x)
                cross = cross + fold(x * prod[was, n * NBLK + k])
                first[c, pl.ds(at, BLOCK), :] = x
                split_store(at, x)
            return norm, cross
        norm, cross = lax.fori_loop(0, NBLK, part, (zero8, zero8))

        if c == 0:
            pass_sum(CHUNKS - 1, 2)
        else:
            pass_sum(CHUNKS + c - 1, 3)

        def group(g, curv):
            r = product_row(g)
            value = product(s, r)

            @pl.when(g == 0)
            def _():
                send_contact(s)
            if c > 0:
                @pl.when(g == 1)
                def _():
                    last_up_copy(0).start()
            return curv + fold(value * first[c, pl.ds(r, FACE), :])
        curv = lax.fori_loop(0, 3, group, zero8)
        start_sum(CHUNKS + c, [row_sum(norm), row_sum(cross), row_sum(curv)])
        if c == 0:
            send_up(s)
            hop_copy(0).start()
        else:
            last_up_copy(1).start()
            hop_copy(0).wait_recv()
            hop_copy(1).start()

    scales = []
    for c in range(CHUNKS):
        if c == CHUNKS - 1:
            pass_sum(CHUNKS + c, 3)
        new_norm, cross, curv = end_sum(CHUNKS + c, 3)
        alpha = alphas[c]
        beta = new_norm / norms[c]
        alpha1 = new_norm / (curv + beta * (2.0 * cross + beta * curvs[c]))
        lead = alpha + alpha1 * beta
        for k in range(1, cols):
            con_copy(c, k).wait_recv()
            con_copy(CHUNKS + c, k).wait_recv()
            con_copy(2 * CHUNKS + c, k).wait_recv()

        def contact_out(k, _):
            r = pl.multiple_of(k * BLOCK, BLOCK)
            r0 = con_in[c, k]
            q0 = con_in[CHUNKS + c, k]
            r1 = r0 - alpha * q0
            out_cm[pl.ds(r, BLOCK), pl.ds(c * COLS, COLS)] = lead * r0 + alpha1 * r1
            out_cr[pl.ds(r, BLOCK), pl.ds(c * COLS, COLS)] = r1 - alpha1 * (con_in[2 * CHUNKS + c, k] + beta * q0)
            return 0
        lax.fori_loop(0, NBLK, contact_out, 0)

        def glue_mult(k, _):
            r = pl.multiple_of(k * BLOCK, BLOCK)
            out_gm[pl.ds(r, BLOCK), pl.ds(c * COLS, COLS)] = (
                lead * field[c, pl.ds(r, BLOCK), :] + alpha1 * first[c, pl.ds(r, BLOCK), :])
            return 0
        lax.fori_loop(0, NBLK, glue_mult, 0)

        if c == 0:
            hop_copy(1).wait_recv()
            hop_copy(2).start()

        scales.append((alpha1, beta))

    for c in range(CHUNKS):
        alpha1, beta = scales[c]
        if c == 0:
            up_copy(2 * CHUNKS).wait_recv()
            hop_copy(2).wait_recv()
        else:
            last_up_copy(0).wait_recv()
            last_up_copy(1).wait_recv()

        def glue_res(k, _):
            r = pl.multiple_of(k * BLOCK, BLOCK)
            x = glue_part(2 * CHUNKS + c, k) + beta * glue_part(CHUNKS + c, k)
            out_gr[pl.ds(r, BLOCK), pl.ds(c * COLS, COLS)] = first[c, pl.ds(r, BLOCK), :] - alpha1 * x
            return 0
        lax.fori_loop(0, NBLK, glue_res, 0)

    for s in range(STEPS):
        if 0 < s < STEPS - 1:
            up_copy(s).wait_send()
        if s < 2 * CHUNKS:
            low_copy(s).wait_send()
        for k in range(1, cols):
            con_copy(s, k).wait_send()
    for n in range(3):
        hop_copy(n).wait_send()
    for h in range(2):
        first_up_copy(h).wait_send()
        last_up_copy(h).wait_send()
    for k in range(1, cols):
        flag_copy(k).wait_send()
    for a in range(2 * CHUNKS):
        for k in range(1, rows):
            sub_copy(a, k).wait_send()
        for k in range(1, cols):
            cont_copy(a, k).wait_send()


def hand_on(*refs):
    ins, outs, sem = refs[:4], refs[4:8], refs[8]
    copies = [pltpu.make_async_copy(a, b, sem.at[n]) for n, (a, b) in enumerate(zip(ins, outs))]
    for copy in copies:
        copy.start()
    for copy in copies:
        copy.wait()


def per_device(schur_matrix, load_vectors, glue_blocks, contact_order, active_flags):
    rows, cols = lax.axis_size("sub"), lax.axis_size("cont")
    any_space = pl.BlockSpec(memory_space=pl.ANY)
    vmem = pl.BlockSpec(memory_space=pltpu.VMEM)
    dma = pltpu.SemaphoreType.DMA
    sums = 2 * CHUNKS
    outs = pl.pallas_call(
        lambda *refs: kernel(rows, cols, *refs),
        out_shape=[pltpu.VMEM((FACE, LOADS), F32)] * 4,
        in_specs=[any_space] * 5,
        out_specs=[vmem] * 4,
        scratch_shapes=[
            pltpu.VMEM((PIECES, PIECE, IFACE), F32),
            pltpu.VMEM((IFACE, IFACE), BF16),
            pltpu.VMEM((IFACE, IFACE), BF16),
            pltpu.VMEM((CHUNKS, IFACE, COLS), F32),
            pltpu.VMEM((IFACE, COLS), BF16),
            pltpu.VMEM((IFACE, COLS), BF16),
            pltpu.VMEM((STEPS, 3 * NBLK, BLOCK, COLS), F32),
            pltpu.VMEM((CHUNKS, IFACE, COLS), F32),
            pltpu.VMEM((NBLK, BLOCK, COLS), F32),
            pltpu.VMEM((2 * CHUNKS, NBLK, BLOCK, COLS), F32),
            pltpu.VMEM((STEPS, NBLK, BLOCK, COLS), F32),
            *[pltpu.VMEM((NBLK, BLOCK, COLS), F32)] * STEPS,
            pltpu.VMEM((2 * CHUNKS, NBLK, BLOCK, COLS), F32),
            pltpu.VMEM((STEPS, NBLK, BLOCK, COLS), F32),
            pltpu.VMEM((cols, 1, FACE), F32),
            pltpu.VMEM((1, FACE), F32),
            pltpu.VMEM((sums, 3, 1, COLS), F32),
            pltpu.VMEM((sums, rows, 3, 1, COLS), F32),
            pltpu.VMEM((sums, 3, 1, COLS), F32),
            pltpu.VMEM((sums, cols, 3, 1, COLS), F32),
            pltpu.SMEM((2, NBLK), jnp.int32),
            pltpu.SMEM((1, NBLK), jnp.int32),
            pltpu.SMEM((1, NBLK), jnp.int32),
            pltpu.VMEM((1, FACE), jnp.int32),
            pltpu.VMEM((ROUND, BLOCK, COLS), F32),
            pltpu.VMEM((ROUND, BLOCK, COLS), F32),
            dma((PIECES,)), dma((CHUNKS,)), dma((3,)),
            dma((2,)), dma((2,)), dma((3,)), dma((3,)), dma((2,)), dma((2,)), dma((STEPS,)), dma((STEPS,)),
            dma((2 * CHUNKS,)), dma((2 * CHUNKS,)),
            dma((STEPS, cols)), dma((STEPS, cols)),
            dma((cols,)), dma((cols,)),
            dma((sums, rows)), dma((sums, rows)),
            dma((sums, cols)), dma((sums, cols)),
        ],
        compiler_params=pltpu.CompilerParams(
            collective_id=0, has_side_effects=True, vmem_limit_bytes=54 * 2**20),
        cost_estimate=pl.CostEstimate(
            flops=3 * 6 * IFACE * IFACE * LOADS, bytes_accessed=4 * (IFACE * IFACE + IFACE * LOADS + 4 * FACE * LOADS),
            transcendentals=0),
    )(
        schur_matrix.reshape(IFACE, IFACE),
        load_vectors.reshape(IFACE, LOADS),
        glue_blocks.reshape(1, NBLK),
        contact_order.reshape(1, NBLK),
        active_flags.reshape(1, FACE),
    )
    outs = pl.pallas_call(
        hand_on,
        out_shape=[jax.ShapeDtypeStruct((FACE, LOADS), F32)] * 4,
        in_specs=[vmem] * 4,
        out_specs=[any_space] * 4,
        scratch_shapes=[dma((4,))],
        compiler_params=pltpu.CompilerParams(vmem_limit_bytes=4 * 2**20),
    )(*outs)
    return tuple(out[None, None] for out in outs)


def solution(mesh):
    return jax.shard_map(
        per_device,
        mesh=mesh,
        in_specs=(
            P("sub", "cont", None, None),
            P("sub", "cont", None, None),
            P("sub", "cont", None),
            P("sub", "cont", None),
            P("sub", "cont", None),
        ),
        out_specs=(P("sub", "cont", None, None),) * 4,
        check_vma=False,
    )
```

```python
import jax
import jax.numpy as jnp
from jax import lax
from jax.experimental import pallas as pl
from jax.experimental.pallas import tpu as pltpu
from jax.sharding import PartitionSpec as P

BLOCK = 64
NBLK = 8
HALF = NBLK // 2
ROUND = 3
RING = 4
EARLY = 2
FACE = BLOCK * NBLK
IFACE = 3 * FACE
LOADS = 512
CHUNKS = 2
COLS = LOADS // CHUNKS
PIECES = 6
PIECE = IFACE // PIECES
STEPS = 3 * CHUNKS
F32 = jnp.float32
BF16 = jnp.bfloat16


def fold(x):
    return jnp.sum(x.reshape(x.shape[0] // 8, 8, COLS), axis=0)


def row_sum(x):
    return jnp.sum(x, axis=0, keepdims=True)


def kernel(
    rows, cols,
    schur, loads, glue_hbm, order_hbm, flags_hbm,
    out_gm, out_cm, out_gr, out_cr,
    stage_s, s_hi, s_lo, field, f_hi, f_lo, prod, first, mask,
    low_out, con_out, up_in_0, up_in_1, up_in_2, up_in_3, up_in_4, up_in_5, low_in, con_in, flag_in, flag_own,
    sum_own, sum_sub, part_own, sum_con, inverse, glue, order, flags, relay_1, relay_2,
    s_sem, l_sem, i_sem,
    last_ss, last_rs, hop_ss, hop_rs, half_ss, half_rs, up_ss, up_rs, low_ss, low_rs, con_ss, con_rs, flag_ss, flag_rs, sub_ss, sub_rs, cont_ss, cont_rs,
):
    up_in = (up_in_0, up_in_1, up_in_2, up_in_3, up_in_4, up_in_5)
    i = lax.axis_index("sub")
    j = lax.axis_index("cont")
    after = lax.rem(i + 1, rows)
    before = lax.rem(i + rows - 1, rows)
    has_before = i > 0
    has_after = i < rows - 1

    barrier = pltpu.get_barrier_semaphore()
    for k in range(1, rows):
        pl.semaphore_signal(barrier, 1, device_id={"sub": lax.rem(i + k, rows)})
    for k in range(1, cols):
        pl.semaphore_signal(barrier, 1, device_id={"cont": lax.rem(j + k, cols)})

    def load_copy(c):
        return pltpu.make_async_copy(loads.at[:, pl.ds(c * COLS, COLS)], field.at[c], l_sem.at[c])

    def piece_row(g):
        n = jnp.where(g == 0, 2, jnp.where(g < 3, g - 1, g))
        return pl.multiple_of(n * PIECE, PIECE)

    def schur_copy(g):
        return pltpu.make_async_copy(schur.at[pl.ds(piece_row(g), PIECE)], stage_s.at[g], s_sem.at[g])

    small_copies = [
        pltpu.make_async_copy(a, b, i_sem.at[n])
        for n, (a, b) in enumerate(((glue_hbm, glue), (order_hbm, order), (flags_hbm, flags)))
    ]
    load_copy(0).start()
    schur_copy(0).start()
    for copy in small_copies:
        copy.start()
    schur_copy(1).start()

    def first_up_copy(h):
        part = pl.ds(NBLK + h * HALF, HALF)
        return pltpu.make_async_remote_copy(
            prod.at[0, part], up_in[0].at[pl.ds(h * HALF, HALF)], half_ss.at[h], half_rs.at[h], device_id={"sub": after})

    def last_up_copy(h):
        s = STEPS - 1
        count = NBLK - EARLY if h else EARLY
        return pltpu.make_async_remote_copy(
            prod.at[s, pl.ds(NBLK + h * EARLY, count)], up_in[s].at[pl.ds(h * EARLY, count)], last_ss.at[h], last_rs.at[h],
            device_id={"sub": after})

    def up_copy(s):
        count = NBLK - ROUND if s == 2 * CHUNKS else NBLK
        return pltpu.make_async_remote_copy(
            prod.at[s, pl.ds(NBLK, count)], up_in[s].at[pl.ds(0, count)], up_ss.at[s], up_rs.at[s],
            device_id={"sub": after})

    ring = lax.rem(i, RING)
    ring_down = i - ring + lax.rem(ring + RING - 1, RING)
    two_down_after = lax.rem(i - ring + lax.rem(ring + 2, RING) + 1, rows)

    def hop_copy(n):
        s = 2 * CHUNKS
        kept = pl.ds(NBLK - ROUND, ROUND)
        src = (prod.at[s, pl.ds(2 * NBLK - ROUND, ROUND)], relay_1, relay_2)[n]
        dst = (relay_1, relay_2, up_in[s].at[kept])[n]
        to = (ring_down, ring_down, two_down_after)[n]
        return pltpu.make_async_remote_copy(src, dst, hop_ss.at[n], hop_rs.at[n], device_id={"sub": to})

    def low_copy(s):
        return pltpu.make_async_remote_copy(
            low_out.at[s], low_in.at[s], low_ss.at[s], low_rs.at[s], device_id={"sub": before})

    def con_copy(s, k):
        t = lax.rem(j + k, cols)
        return pltpu.make_async_remote_copy(
            con_out.at[s, t], con_in.at[s, j], con_ss.at[s, k], con_rs.at[s, k], device_id={"cont": t})

    def flag_copy(k):
        return pltpu.make_async_remote_copy(
            flag_own, flag_in.at[j], flag_ss.at[k], flag_rs.at[k], device_id={"cont": lax.rem(j + k, cols)})

    def held(a):
        return pl.ds(0, 2 if a < CHUNKS else 3)

    def sub_copy(a, k):
        return pltpu.make_async_remote_copy(
            sum_own.at[a, held(a)], sum_sub.at[a, i, held(a)], sub_ss.at[a, k], sub_rs.at[a, k], device_id={"sub": lax.rem(i + k, rows)})

    def cont_copy(a, k):
        return pltpu.make_async_remote_copy(
            part_own.at[a, held(a)], sum_con.at[a, j, held(a)], cont_ss.at[a, k], cont_rs.at[a, k], device_id={"cont": lax.rem(j + k, cols)})

    def make_inverse():
        for n, ref in enumerate((glue, order)):
            for m in range(NBLK):
                found = jnp.int32(0)
                for k in range(1, NBLK):
                    found = jnp.maximum(found, k * (ref[0, k] == m).astype(jnp.int32))
                inverse[n, m] = found

    def split_store(r, x):
        hi = x.astype(BF16)
        f_hi[pl.ds(r, x.shape[0]), :] = hi
        f_lo[pl.ds(r, x.shape[0]), :] = (x - hi.astype(F32)).astype(BF16)

    def product(s, r, size=FACE):
        a_hi = s_hi[pl.ds(r, size), :]
        a_lo = s_lo[pl.ds(r, size), :]
        value = jnp.dot(a_hi, f_hi[...], preferred_element_type=F32)
        value = value + jnp.dot(a_hi, f_lo[...], preferred_element_type=F32)
        value = value + jnp.dot(a_lo, f_hi[...], preferred_element_type=F32)
        prod[s, pl.ds(lax.div(r, BLOCK), size // BLOCK)] = value.reshape(size // BLOCK, BLOCK, COLS)
        return value

    def group_row(g):
        return pl.multiple_of(jnp.where(g == 0, FACE, jnp.where(g == 1, 0, 2 * FACE)), FACE)

    def product_row(g):
        return pl.multiple_of((2 - g) * FACE, FACE)

    def send_up(s):
        up_copy(s).start()

    def send_low(s):
        def move(m, _):
            low_out[s, m] = prod[s, inverse[0, m]]
            return 0
        lax.fori_loop(0, NBLK, move, 0)
        low_copy(s).start()

    def send_contact(s):
        def move(t, _):
            con_out[s, t] = prod[s, 2 * NBLK + order[0, t]] * mask[t]
            return 0
        lax.fori_loop(0, NBLK, move, 0)
        for k in range(1, cols):
            con_copy(s, k).start()
        con_in[s, j] = con_out[s, j]

    def glue_part(s, k):
        return prod[s, k] - jnp.where(has_before, up_in[s][glue[0, k]], 0.0)

    def upper_part(s, m):
        return jnp.where(has_after, prod[s, NBLK + m] - low_in[s, m], 0.0)

    def contact_part(s, k):
        return prod[s, 2 * NBLK + k] * mask[inverse[1, k]]

    def start_sum(a, values):
        for n, v in enumerate(values):
            sum_own[a, n] = v
            sum_sub[a, i, n] = v
        for k in range(1, rows):
            sub_copy(a, k).start()

    def pass_sum(a, count):
        for k in range(1, rows):
            sub_copy(a, k).wait_recv()
        for n in range(count):
            v = sum_sub[a, 0, n]
            for k in range(1, rows):
                v = v + sum_sub[a, k, n]
            part_own[a, n] = v
            sum_con[a, j, n] = v
        for k in range(1, cols):
            cont_copy(a, k).start()

    def end_sum(a, count):
        for k in range(1, cols):
            cont_copy(a, k).wait_recv()
        totals = []
        for n in range(count):
            v = sum_con[a, 0, n]
            for k in range(1, cols):
                v = v + sum_con[a, k, n]
            totals.append(v)
        return totals

    zero8 = jnp.zeros((8, COLS), F32)
    zero1 = jnp.zeros((1, COLS), F32)

    def split_loads(c):
        def part(n, _):
            r = pl.multiple_of(n * 128, 128)
            split_store(r, field[c, pl.ds(r, 128), :])
            return 0
        lax.fori_loop(0, IFACE // 128, part, 0)

    load_copy(0).wait()
    schur_copy(2).start()
    split_loads(0)

    def piece(g, _):
        r = piece_row(g)
        schur_copy(g).wait()

        @pl.when(g < PIECES - 3)
        def _():
            schur_copy(g + 3).start()
        x = stage_s[g]
        hi = x.astype(BF16)
        s_hi[pl.ds(r, PIECE), :] = hi
        s_lo[pl.ds(r, PIECE), :] = (x - hi.astype(F32)).astype(BF16)
        product(0, r, PIECE)

        @pl.when(g == 0)
        def _():
            pl.semaphore_wait(barrier, rows - 1 + cols - 1)
            first_up_copy(0).start()
            for copy in small_copies:
                copy.wait()
            make_inverse()

        @pl.when(g == 2)
        def _():
            send_low(0)

        @pl.when(g == 3)
        def _():
            first_up_copy(1).start()
            for c in range(1, CHUNKS):
                load_copy(c).start()
        return 0
    lax.fori_loop(0, PIECES, piece, 0)
    flag_own[...] = flags[...].astype(F32)
    for k in range(1, cols):
        flag_copy(k).start()
    flag_in[j] = flag_own[...]

    for c in range(1, CHUNKS):
        load_copy(c).wait()
        split_loads(c)

        def group(g, _):
            product(c, group_row(g))
            return 0
        lax.fori_loop(0, 3, group, 0)
        send_up(c)
        send_low(c)

    for k in range(1, cols):
        flag_copy(k).wait_recv()
    lane = lax.broadcasted_iota(jnp.int32, (BLOCK, FACE), 1)
    want = lax.broadcasted_iota(jnp.int32, (BLOCK, FACE), 0) + j * BLOCK

    def mask_of(t, _):
        picked = jnp.where(lane == want, flag_in[t], 0.0)
        mask[t] = jnp.broadcast_to(jnp.sum(picked, axis=1, keepdims=True), (BLOCK, COLS))
        return 0
    lax.fori_loop(0, NBLK, mask_of, 0)

    for c in range(CHUNKS):
        send_contact(c)

    for c in range(CHUNKS):
        was, s = c, CHUNKS + c
        if c == 0:
            first_up_copy(0).wait_recv()
            first_up_copy(1).wait_recv()
        else:
            up_copy(was).wait_recv()
        low_copy(was).wait_recv()

        def part(k, norm):
            r = pl.multiple_of(k * BLOCK, BLOCK)
            x = glue_part(was, k)
            norm = norm + fold(x * x)
            field[c, pl.ds(r, BLOCK), :] = x
            split_store(r, x)
            x = upper_part(was, k)
            field[c, pl.ds(pl.multiple_of(FACE + r, BLOCK), BLOCK), :] = x
            split_store(pl.multiple_of(FACE + r, BLOCK), x)
            x = contact_part(was, k)
            norm = norm + fold(x * x)
            field[c, pl.ds(pl.multiple_of(2 * FACE + r, BLOCK), BLOCK), :] = x
            split_store(pl.multiple_of(2 * FACE + r, BLOCK), x)
            return norm
        norm = lax.fori_loop(0, NBLK, part, zero8)

        if c > 0:
            pass_sum(c - 1, 2)

        def group(g, curv):
            r = product_row(g)
            value = product(s, r)

            @pl.when(g == 0)
            def _():
                send_contact(s)
            return curv + fold(value * field[c, pl.ds(r, FACE), :])
        curv = lax.fori_loop(0, 3, group, zero8)
        start_sum(c, [row_sum(norm), row_sum(curv)])
        send_up(s)
        send_low(s)

    alphas, norms, curvs = [], [], []
    for c in range(CHUNKS):
        was, s = CHUNKS + c, 2 * CHUNKS + c
        up_copy(was).wait_recv()
        low_copy(was).wait_recv()
        total_norm, total_curv = end_sum(c, 2)
        alpha = total_norm / total_curv
        alphas.append(alpha)
        norms.append(total_norm)
        curvs.append(total_curv)

        def part(k, carry):
            norm, cross = carry
            r = pl.multiple_of(k * BLOCK, BLOCK)
            for n, of in enumerate((glue_part, upper_part, contact_part)):
                at = pl.multiple_of(n * FACE + r, BLOCK)
                x = field[c, pl.ds(at, BLOCK), :] - alpha * of(was, k)
                if n != 1:
                    norm = norm + fold(x * x)
                cross = cross + fold(x * prod[was, n * NBLK + k])
                first[c, pl.ds(at, BLOCK), :] = x
                split_store(at, x)
            return norm, cross
        norm, cross = lax.fori_loop(0, NBLK, part, (zero8, zero8))

        if c == 0:
            pass_sum(CHUNKS - 1, 2)
        else:
            pass_sum(CHUNKS + c - 1, 3)

        def group(g, curv):
            r = product_row(g)
            value = product(s, r)

            @pl.when(g == 0)
            def _():
                send_contact(s)
            if c > 0:
                @pl.when(g == 1)
                def _():
                    last_up_copy(0).start()
            return curv + fold(value * first[c, pl.ds(r, FACE), :])
        curv = lax.fori_loop(0, 3, group, zero8)
        start_sum(CHUNKS + c, [row_sum(norm), row_sum(cross), row_sum(curv)])
        if c == 0:
            send_up(s)
            hop_copy(0).start()
        else:
            last_up_copy(1).start()
            hop_copy(0).wait_recv()
            hop_copy(1).start()

    scales = []
    for c in range(CHUNKS):
        new_norm, cross, curv = end_sum(CHUNKS + c, 3)
        alpha = alphas[c]
        beta = new_norm / norms[c]
        alpha1 = new_norm / (curv + beta * (2.0 * cross + beta * curvs[c]))
        lead = alpha + alpha1 * beta
        for k in range(1, cols):
            con_copy(c, k).wait_recv()
            con_copy(CHUNKS + c, k).wait_recv()
            con_copy(2 * CHUNKS + c, k).wait_recv()

        def contact_out(k, _):
            r = pl.multiple_of(k * BLOCK, BLOCK)
            r0 = con_in[c, k]
            q0 = con_in[CHUNKS + c, k]
            r1 = r0 - alpha * q0
            out_cm[pl.ds(r, BLOCK), pl.ds(c * COLS, COLS)] = lead * r0 + alpha1 * r1
            out_cr[pl.ds(r, BLOCK), pl.ds(c * COLS, COLS)] = r1 - alpha1 * (con_in[2 * CHUNKS + c, k] + beta * q0)
            return 0
        lax.fori_loop(0, NBLK, contact_out, 0)

        def glue_mult(k, _):
            r = pl.multiple_of(k * BLOCK, BLOCK)
            out_gm[pl.ds(r, BLOCK), pl.ds(c * COLS, COLS)] = (
                lead * field[c, pl.ds(r, BLOCK), :] + alpha1 * first[c, pl.ds(r, BLOCK), :])
            return 0
        lax.fori_loop(0, NBLK, glue_mult, 0)

        if c == 0:
            pass_sum(STEPS - CHUNKS - 1, 3)
            hop_copy(1).wait_recv()
            hop_copy(2).start()

        scales.append((alpha1, beta))

    for c in range(CHUNKS):
        alpha1, beta = scales[c]
        if c == 0:
            up_copy(2 * CHUNKS).wait_recv()
            hop_copy(2).wait_recv()
        else:
            last_up_copy(0).wait_recv()
            last_up_copy(1).wait_recv()

        def glue_res(k, _):
            r = pl.multiple_of(k * BLOCK, BLOCK)
            x = glue_part(2 * CHUNKS + c, k) + beta * glue_part(CHUNKS + c, k)
            out_gr[pl.ds(r, BLOCK), pl.ds(c * COLS, COLS)] = first[c, pl.ds(r, BLOCK), :] - alpha1 * x
            return 0
        lax.fori_loop(0, NBLK, glue_res, 0)

    for s in range(STEPS):
        if 0 < s < STEPS - 1:
            up_copy(s).wait_send()
        if s < 2 * CHUNKS:
            low_copy(s).wait_send()
        for k in range(1, cols):
            con_copy(s, k).wait_send()
    for n in range(3):
        hop_copy(n).wait_send()
    for h in range(2):
        first_up_copy(h).wait_send()
        last_up_copy(h).wait_send()
    for k in range(1, cols):
        flag_copy(k).wait_send()
    for a in range(2 * CHUNKS):
        for k in range(1, rows):
            sub_copy(a, k).wait_send()
        for k in range(1, cols):
            cont_copy(a, k).wait_send()


def hand_on(*refs):
    ins, outs, sem = refs[:4], refs[4:8], refs[8]
    copies = [pltpu.make_async_copy(a, b, sem.at[n]) for n, (a, b) in enumerate(zip(ins, outs))]
    for copy in copies:
        copy.start()
    for copy in copies:
        copy.wait()


def per_device(schur_matrix, load_vectors, glue_blocks, contact_order, active_flags):
    rows, cols = lax.axis_size("sub"), lax.axis_size("cont")
    any_space = pl.BlockSpec(memory_space=pl.ANY)
    vmem = pl.BlockSpec(memory_space=pltpu.VMEM)
    dma = pltpu.SemaphoreType.DMA
    sums = 2 * CHUNKS
    outs = pl.pallas_call(
        lambda *refs: kernel(rows, cols, *refs),
        out_shape=[pltpu.VMEM((FACE, LOADS), F32)] * 4,
        in_specs=[any_space] * 5,
        out_specs=[vmem] * 4,
        scratch_shapes=[
            pltpu.VMEM((PIECES, PIECE, IFACE), F32),
            pltpu.VMEM((IFACE, IFACE), BF16),
            pltpu.VMEM((IFACE, IFACE), BF16),
            pltpu.VMEM((CHUNKS, IFACE, COLS), F32),
            pltpu.VMEM((IFACE, COLS), BF16),
            pltpu.VMEM((IFACE, COLS), BF16),
            pltpu.VMEM((STEPS, 3 * NBLK, BLOCK, COLS), F32),
            pltpu.VMEM((CHUNKS, IFACE, COLS), F32),
            pltpu.VMEM((NBLK, BLOCK, COLS), F32),
            pltpu.VMEM((2 * CHUNKS, NBLK, BLOCK, COLS), F32),
            pltpu.VMEM((STEPS, NBLK, BLOCK, COLS), F32),
            *[pltpu.VMEM((NBLK, BLOCK, COLS), F32)] * STEPS,
            pltpu.VMEM((2 * CHUNKS, NBLK, BLOCK, COLS), F32),
            pltpu.VMEM((STEPS, NBLK, BLOCK, COLS), F32),
            pltpu.VMEM((cols, 1, FACE), F32),
            pltpu.VMEM((1, FACE), F32),
            pltpu.VMEM((sums, 3, 1, COLS), F32),
            pltpu.VMEM((sums, rows, 3, 1, COLS), F32),
            pltpu.VMEM((sums, 3, 1, COLS), F32),
            pltpu.VMEM((sums, cols, 3, 1, COLS), F32),
            pltpu.SMEM((2, NBLK), jnp.int32),
            pltpu.SMEM((1, NBLK), jnp.int32),
            pltpu.SMEM((1, NBLK), jnp.int32),
            pltpu.VMEM((1, FACE), jnp.int32),
            pltpu.VMEM((ROUND, BLOCK, COLS), F32),
            pltpu.VMEM((ROUND, BLOCK, COLS), F32),
            dma((PIECES,)), dma((CHUNKS,)), dma((3,)),
            dma((2,)), dma((2,)), dma((3,)), dma((3,)), dma((2,)), dma((2,)), dma((STEPS,)), dma((STEPS,)),
            dma((2 * CHUNKS,)), dma((2 * CHUNKS,)),
            dma((STEPS, cols)), dma((STEPS, cols)),
            dma((cols,)), dma((cols,)),
            dma((sums, rows)), dma((sums, rows)),
            dma((sums, cols)), dma((sums, cols)),
        ],
        compiler_params=pltpu.CompilerParams(
            collective_id=0, has_side_effects=True, vmem_limit_bytes=54 * 2**20),
        cost_estimate=pl.CostEstimate(
            flops=3 * 6 * IFACE * IFACE * LOADS, bytes_accessed=4 * (IFACE * IFACE + IFACE * LOADS + 4 * FACE * LOADS),
            transcendentals=0),
    )(
        schur_matrix.reshape(IFACE, IFACE),
        load_vectors.reshape(IFACE, LOADS),
        glue_blocks.reshape(1, NBLK),
        contact_order.reshape(1, NBLK),
        active_flags.reshape(1, FACE),
    )
    outs = pl.pallas_call(
        hand_on,
        out_shape=[jax.ShapeDtypeStruct((FACE, LOADS), F32)] * 4,
        in_specs=[vmem] * 4,
        out_specs=[any_space] * 4,
        scratch_shapes=[dma((4,))],
        compiler_params=pltpu.CompilerParams(vmem_limit_bytes=4 * 2**20),
    )(*outs)
    return tuple(out[None, None] for out in outs)


def solution(mesh):
    return jax.shard_map(
        per_device,
        mesh=mesh,
        in_specs=(
            P("sub", "cont", None, None),
            P("sub", "cont", None, None),
            P("sub", "cont", None),
            P("sub", "cont", None),
            P("sub", "cont", None),
        ),
        out_specs=(P("sub", "cont", None, None),) * 4,
        check_vma=False,
    )
```

```python
import jax
import jax.numpy as jnp
from jax import lax
from jax.experimental import pallas as pl
from jax.experimental.pallas import tpu as pltpu
from jax.sharding import PartitionSpec as P

BLOCK = 64
NBLK = 8
HALF = NBLK // 2
ROUND = 3
RING = 4
EARLY = 2
FACE = BLOCK * NBLK
IFACE = 3 * FACE
LOADS = 512
CHUNKS = 2
COLS = LOADS // CHUNKS
PIECES = 6
PIECE = IFACE // PIECES
STEPS = 3 * CHUNKS
F32 = jnp.float32
BF16 = jnp.bfloat16


def fold(x):
    return jnp.sum(x.reshape(x.shape[0] // 8, 8, COLS), axis=0)


def row_sum(x):
    return jnp.sum(x, axis=0, keepdims=True)


def kernel(
    rows, cols,
    schur, loads, glue_hbm, order_hbm, flags_hbm,
    out_gm, out_cm, out_gr, out_cr,
    stage_s, s_hi, s_lo, field, f_hi, f_lo, prod, first, mask,
    low_out, con_out, up_in_0, up_in_1, up_in_2, up_in_3, up_in_4, up_in_5, low_in, con_in, flag_in, flag_own,
    sum_own, sum_sub, part_own, sum_con, inverse, glue, order, flags, relay_1, relay_2,
    s_sem, l_sem, i_sem,
    last_ss, last_rs, hop_ss, hop_rs, half_ss, half_rs, up_ss, up_rs, low_ss, low_rs, con_ss, con_rs, flag_ss, flag_rs, sub_ss, sub_rs, cont_ss, cont_rs,
):
    up_in = (up_in_0, up_in_1, up_in_2, up_in_3, up_in_4, up_in_5)
    i = lax.axis_index("sub")
    j = lax.axis_index("cont")
    after = lax.rem(i + 1, rows)
    before = lax.rem(i + rows - 1, rows)
    has_before = i > 0
    has_after = i < rows - 1

    def load_copy(c):
        return pltpu.make_async_copy(loads.at[:, pl.ds(c * COLS, COLS)], field.at[c], l_sem.at[c])

    def piece_row(g):
        n = jnp.where(g == 0, 2, jnp.where(g < 3, g - 1, g))
        return pl.multiple_of(n * PIECE, PIECE)

    def schur_copy(g):
        return pltpu.make_async_copy(schur.at[pl.ds(piece_row(g), PIECE)], stage_s.at[g], s_sem.at[g])

    small_copies = [
        pltpu.make_async_copy(a, b, i_sem.at[n])
        for n, (a, b) in enumerate(((glue_hbm, glue), (order_hbm, order), (flags_hbm, flags)))
    ]
    load_copy(0).start()
    schur_copy(0).start()
    for copy in small_copies:
        copy.start()
    schur_copy(1).start()

    barrier = pltpu.get_barrier_semaphore()
    for k in range(1, rows):
        pl.semaphore_signal(barrier, 1, device_id={"sub": lax.rem(i + k, rows)})
    for k in range(1, cols):
        pl.semaphore_signal(barrier, 1, device_id={"cont": lax.rem(j + k, cols)})

    def first_up_copy(h):
        part = pl.ds(NBLK + h * HALF, HALF)
        return pltpu.make_async_remote_copy(
            prod.at[0, part], up_in[0].at[pl.ds(h * HALF, HALF)], half_ss.at[h], half_rs.at[h], device_id={"sub": after})

    def last_up_copy(h):
        s = STEPS - 1
        count = NBLK - EARLY if h else EARLY
        return pltpu.make_async_remote_copy(
            prod.at[s, pl.ds(NBLK + h * EARLY, count)], up_in[s].at[pl.ds(h * EARLY, count)], last_ss.at[h], last_rs.at[h],
            device_id={"sub": after})

    def up_copy(s):
        count = NBLK - ROUND if s == 2 * CHUNKS else NBLK
        return pltpu.make_async_remote_copy(
            prod.at[s, pl.ds(NBLK, count)], up_in[s].at[pl.ds(0, count)], up_ss.at[s], up_rs.at[s],
            device_id={"sub": after})

    ring = lax.rem(i, RING)
    ring_down = i - ring + lax.rem(ring + RING - 1, RING)
    two_down_after = lax.rem(i - ring + lax.rem(ring + 2, RING) + 1, rows)

    def hop_copy(n):
        s = 2 * CHUNKS
        kept = pl.ds(NBLK - ROUND, ROUND)
        src = (prod.at[s, pl.ds(2 * NBLK - ROUND, ROUND)], relay_1, relay_2)[n]
        dst = (relay_1, relay_2, up_in[s].at[kept])[n]
        to = (ring_down, ring_down, two_down_after)[n]
        return pltpu.make_async_remote_copy(src, dst, hop_ss.at[n], hop_rs.at[n], device_id={"sub": to})

    def low_copy(s):
        return pltpu.make_async_remote_copy(
            low_out.at[s], low_in.at[s], low_ss.at[s], low_rs.at[s], device_id={"sub": before})

    def con_copy(s, k):
        t = lax.rem(j + k, cols)
        return pltpu.make_async_remote_copy(
            con_out.at[s, t], con_in.at[s, j], con_ss.at[s, k], con_rs.at[s, k], device_id={"cont": t})

    def flag_copy(k):
        return pltpu.make_async_remote_copy(
            flag_own, flag_in.at[j], flag_ss.at[k], flag_rs.at[k], device_id={"cont": lax.rem(j + k, cols)})

    def held(a):
        return pl.ds(0, 2 if a < CHUNKS else 3)

    def sub_copy(a, k):
        return pltpu.make_async_remote_copy(
            sum_own.at[a, held(a)], sum_sub.at[a, i, held(a)], sub_ss.at[a, k], sub_rs.at[a, k], device_id={"sub": lax.rem(i + k, rows)})

    def cont_copy(a, k):
        return pltpu.make_async_remote_copy(
            part_own.at[a, held(a)], sum_con.at[a, j, held(a)], cont_ss.at[a, k], cont_rs.at[a, k], device_id={"cont": lax.rem(j + k, cols)})

    def make_inverse():
        for n, ref in enumerate((glue, order)):
            for m in range(NBLK):
                found = jnp.int32(0)
                for k in range(1, NBLK):
                    found = jnp.maximum(found, k * (ref[0, k] == m).astype(jnp.int32))
                inverse[n, m] = found

    def split_store(r, x):
        hi = x.astype(BF16)
        f_hi[pl.ds(r, x.shape[0]), :] = hi
        f_lo[pl.ds(r, x.shape[0]), :] = (x - hi.astype(F32)).astype(BF16)

    def product(s, r, size=FACE):
        a_hi = s_hi[pl.ds(r, size), :]
        a_lo = s_lo[pl.ds(r, size), :]
        value = jnp.dot(a_hi, f_hi[...], preferred_element_type=F32)
        value = value + jnp.dot(a_hi, f_lo[...], preferred_element_type=F32)
        value = value + jnp.dot(a_lo, f_hi[...], preferred_element_type=F32)
        prod[s, pl.ds(lax.div(r, BLOCK), size // BLOCK)] = value.reshape(size // BLOCK, BLOCK, COLS)
        return value

    def group_row(g):
        return pl.multiple_of(jnp.where(g == 0, FACE, jnp.where(g == 1, 0, 2 * FACE)), FACE)

    def product_row(g):
        return pl.multiple_of((2 - g) * FACE, FACE)

    def send_up(s):
        up_copy(s).start()

    def send_low(s):
        def move(m, _):
            low_out[s, m] = prod[s, inverse[0, m]]
            return 0
        lax.fori_loop(0, NBLK, move, 0)
        low_copy(s).start()

    def send_contact(s):
        def move(t, _):
            con_out[s, t] = prod[s, 2 * NBLK + order[0, t]] * mask[t]
            return 0
        lax.fori_loop(0, NBLK, move, 0)
        for k in range(1, cols):
            con_copy(s, k).start()
        con_in[s, j] = con_out[s, j]

    def glue_part(s, k):
        return prod[s, k] - jnp.where(has_before, up_in[s][glue[0, k]], 0.0)

    def upper_part(s, m):
        return jnp.where(has_after, prod[s, NBLK + m] - low_in[s, m], 0.0)

    def contact_part(s, k):
        return prod[s, 2 * NBLK + k] * mask[inverse[1, k]]

    def start_sum(a, values):
        for n, v in enumerate(values):
            sum_own[a, n] = v
            sum_sub[a, i, n] = v
        for k in range(1, rows):
            sub_copy(a, k).start()

    def pass_sum(a, count):
        for k in range(1, rows):
            sub_copy(a, k).wait_recv()
        for n in range(count):
            v = sum_sub[a, 0, n]
            for k in range(1, rows):
                v = v + sum_sub[a, k, n]
            part_own[a, n] = v
            sum_con[a, j, n] = v
        for k in range(1, cols):
            cont_copy(a, k).start()

    def end_sum(a, count):
        for k in range(1, cols):
            cont_copy(a, k).wait_recv()
        totals = []
        for n in range(count):
            v = sum_con[a, 0, n]
            for k in range(1, cols):
                v = v + sum_con[a, k, n]
            totals.append(v)
        return totals

    zero8 = jnp.zeros((8, COLS), F32)
    zero1 = jnp.zeros((1, COLS), F32)

    def split_loads(c):
        def part(n, _):
            r = pl.multiple_of(n * 128, 128)
            split_store(r, field[c, pl.ds(r, 128), :])
            return 0
        lax.fori_loop(0, IFACE // 128, part, 0)

    load_copy(0).wait()
    schur_copy(2).start()
    split_loads(0)

    def piece(g, _):
        r = piece_row(g)
        schur_copy(g).wait()

        @pl.when(g < PIECES - 3)
        def _():
            schur_copy(g + 3).start()
        x = stage_s[g]
        hi = x.astype(BF16)
        s_hi[pl.ds(r, PIECE), :] = hi
        s_lo[pl.ds(r, PIECE), :] = (x - hi.astype(F32)).astype(BF16)
        product(0, r, PIECE)

        @pl.when(g == 0)
        def _():
            pl.semaphore_wait(barrier, rows - 1 + cols - 1)
            first_up_copy(0).start()
            for copy in small_copies:
                copy.wait()
            make_inverse()

        @pl.when(g == 2)
        def _():
            send_low(0)

        @pl.when(g == 3)
        def _():
            first_up_copy(1).start()
            for c in range(1, CHUNKS):
                load_copy(c).start()
        return 0
    lax.fori_loop(0, PIECES, piece, 0)
    flag_own[...] = flags[...].astype(F32)
    for k in range(1, cols):
        flag_copy(k).start()
    flag_in[j] = flag_own[...]

    for c in range(1, CHUNKS):
        load_copy(c).wait()
        split_loads(c)

        def group(g, _):
            product(c, group_row(g))
            return 0
        lax.fori_loop(0, 3, group, 0)
        send_up(c)
        send_low(c)

    for k in range(1, cols):
        flag_copy(k).wait_recv()
    lane = lax.broadcasted_iota(jnp.int32, (BLOCK, FACE), 1)
    want = lax.broadcasted_iota(jnp.int32, (BLOCK, FACE), 0) + j * BLOCK

    def mask_of(t, _):
        picked = jnp.where(lane == want, flag_in[t], 0.0)
        mask[t] = jnp.broadcast_to(jnp.sum(picked, axis=1, keepdims=True), (BLOCK, COLS))
        return 0
    lax.fori_loop(0, NBLK, mask_of, 0)

    for c in range(CHUNKS):
        send_contact(c)

    for c in range(CHUNKS):
        was, s = c, CHUNKS + c
        if c == 0:
            first_up_copy(0).wait_recv()
            first_up_copy(1).wait_recv()
        else:
            up_copy(was).wait_recv()
        low_copy(was).wait_recv()

        def part(k, norm):
            r = pl.multiple_of(k * BLOCK, BLOCK)
            x = glue_part(was, k)
            norm = norm + fold(x * x)
            field[c, pl.ds(r, BLOCK), :] = x
            split_store(r, x)
            x = upper_part(was, k)
            field[c, pl.ds(pl.multiple_of(FACE + r, BLOCK), BLOCK), :] = x
            split_store(pl.multiple_of(FACE + r, BLOCK), x)
            x = contact_part(was, k)
            norm = norm + fold(x * x)
            field[c, pl.ds(pl.multiple_of(2 * FACE + r, BLOCK), BLOCK), :] = x
            split_store(pl.multiple_of(2 * FACE + r, BLOCK), x)
            return norm
        norm = lax.fori_loop(0, NBLK, part, zero8)

        if c > 0:
            pass_sum(c - 1, 2)

        def group(g, curv):
            r = product_row(g)
            value = product(s, r)

            @pl.when(g == 0)
            def _():
                send_contact(s)
            return curv + fold(value * field[c, pl.ds(r, FACE), :])
        curv = lax.fori_loop(0, 3, group, zero8)
        start_sum(c, [row_sum(norm), row_sum(curv)])
        send_up(s)
        send_low(s)

    alphas, norms, curvs = [], [], []
    for c in range(CHUNKS):
        was, s = CHUNKS + c, 2 * CHUNKS + c
        up_copy(was).wait_recv()
        low_copy(was).wait_recv()
        total_norm, total_curv = end_sum(c, 2)
        alpha = total_norm / total_curv
        alphas.append(alpha)
        norms.append(total_norm)
        curvs.append(total_curv)

        def part(k, carry):
            norm, cross = carry
            r = pl.multiple_of(k * BLOCK, BLOCK)
            for n, of in enumerate((glue_part, upper_part, contact_part)):
                at = pl.multiple_of(n * FACE + r, BLOCK)
                x = field[c, pl.ds(at, BLOCK), :] - alpha * of(was, k)
                if n != 1:
                    norm = norm + fold(x * x)
                cross = cross + fold(x * prod[was, n * NBLK + k])
                first[c, pl.ds(at, BLOCK), :] = x
                split_store(at, x)
            return norm, cross
        norm, cross = lax.fori_loop(0, NBLK, part, (zero8, zero8))

        if c == 0:
            pass_sum(CHUNKS - 1, 2)
        else:
            pass_sum(CHUNKS + c - 1, 3)

        def group(g, curv):
            r = product_row(g)
            value = product(s, r)

            @pl.when(g == 0)
            def _():
                send_contact(s)
            if c > 0:
                @pl.when(g == 1)
                def _():
                    last_up_copy(0).start()
            return curv + fold(value * first[c, pl.ds(r, FACE), :])
        curv = lax.fori_loop(0, 3, group, zero8)
        start_sum(CHUNKS + c, [row_sum(norm), row_sum(cross), row_sum(curv)])
        if c == 0:
            send_up(s)
            hop_copy(0).start()
        else:
            last_up_copy(1).start()
            hop_copy(0).wait_recv()
            hop_copy(1).start()

    def end_earlier_sends():
        for s in range(STEPS):
            if 0 < s < STEPS - 1:
                up_copy(s).wait_send()
            if s < 2 * CHUNKS:
                low_copy(s).wait_send()
            for k in range(1, cols):
                con_copy(s, k).wait_send()
        for n in range(2):
            hop_copy(n).wait_send()
        for h in range(2):
            first_up_copy(h).wait_send()
        for k in range(1, cols):
            flag_copy(k).wait_send()
        for a in range(2 * CHUNKS):
            for k in range(1, rows):
                sub_copy(a, k).wait_send()
            for k in range(1, cols):
                cont_copy(a, k).wait_send()

    scales = []
    for c in range(CHUNKS):
        new_norm, cross, curv = end_sum(CHUNKS + c, 3)
        alpha = alphas[c]
        beta = new_norm / norms[c]
        alpha1 = new_norm / (curv + beta * (2.0 * cross + beta * curvs[c]))
        lead = alpha + alpha1 * beta
        for k in range(1, cols):
            con_copy(c, k).wait_recv()
            con_copy(CHUNKS + c, k).wait_recv()
            con_copy(2 * CHUNKS + c, k).wait_recv()

        def contact_out(k, _):
            r = pl.multiple_of(k * BLOCK, BLOCK)
            r0 = con_in[c, k]
            q0 = con_in[CHUNKS + c, k]
            r1 = r0 - alpha * q0
            out_cm[pl.ds(r, BLOCK), pl.ds(c * COLS, COLS)] = lead * r0 + alpha1 * r1
            out_cr[pl.ds(r, BLOCK), pl.ds(c * COLS, COLS)] = r1 - alpha1 * (con_in[2 * CHUNKS + c, k] + beta * q0)
            return 0
        lax.fori_loop(0, NBLK, contact_out, 0)

        def glue_mult(k, _):
            r = pl.multiple_of(k * BLOCK, BLOCK)
            out_gm[pl.ds(r, BLOCK), pl.ds(c * COLS, COLS)] = (
                lead * field[c, pl.ds(r, BLOCK), :] + alpha1 * first[c, pl.ds(r, BLOCK), :])
            return 0
        lax.fori_loop(0, NBLK, glue_mult, 0)

        if c == 0:
            pass_sum(STEPS - CHUNKS - 1, 3)
            hop_copy(1).wait_recv()
            hop_copy(2).start()

        scales.append((alpha1, beta))

    for c in range(CHUNKS):
        alpha1, beta = scales[c]
        if c == 0:
            up_copy(2 * CHUNKS).wait_recv()
            hop_copy(2).wait_recv()
        else:
            end_earlier_sends()
            last_up_copy(0).wait_recv()
            last_up_copy(1).wait_recv()

        def glue_res(k, _):
            r = pl.multiple_of(k * BLOCK, BLOCK)
            x = glue_part(2 * CHUNKS + c, k) + beta * glue_part(CHUNKS + c, k)
            out_gr[pl.ds(r, BLOCK), pl.ds(c * COLS, COLS)] = first[c, pl.ds(r, BLOCK), :] - alpha1 * x
            return 0
        lax.fori_loop(0, NBLK, glue_res, 0)

    last_up_copy(0).wait_send()
    last_up_copy(1).wait_send()
    hop_copy(2).wait_send()


def hand_on(*refs):
    ins, outs, sem = refs[:4], refs[4:8], refs[8]
    copies = [pltpu.make_async_copy(a, b, sem.at[n]) for n, (a, b) in enumerate(zip(ins, outs))]
    for copy in copies:
        copy.start()
    for copy in copies:
        copy.wait()


def per_device(schur_matrix, load_vectors, glue_blocks, contact_order, active_flags):
    rows, cols = lax.axis_size("sub"), lax.axis_size("cont")
    any_space = pl.BlockSpec(memory_space=pl.ANY)
    vmem = pl.BlockSpec(memory_space=pltpu.VMEM)
    dma = pltpu.SemaphoreType.DMA
    sums = 2 * CHUNKS
    outs = pl.pallas_call(
        lambda *refs: kernel(rows, cols, *refs),
        out_shape=[pltpu.VMEM((FACE, LOADS), F32)] * 4,
        in_specs=[any_space] * 5,
        out_specs=[vmem] * 4,
        scratch_shapes=[
            pltpu.VMEM((PIECES, PIECE, IFACE), F32),
            pltpu.VMEM((IFACE, IFACE), BF16),
            pltpu.VMEM((IFACE, IFACE), BF16),
            pltpu.VMEM((CHUNKS, IFACE, COLS), F32),
            pltpu.VMEM((IFACE, COLS), BF16),
            pltpu.VMEM((IFACE, COLS), BF16),
            pltpu.VMEM((STEPS, 3 * NBLK, BLOCK, COLS), F32),
            pltpu.VMEM((CHUNKS, IFACE, COLS), F32),
            pltpu.VMEM((NBLK, BLOCK, COLS), F32),
            pltpu.VMEM((2 * CHUNKS, NBLK, BLOCK, COLS), F32),
            pltpu.VMEM((STEPS, NBLK, BLOCK, COLS), F32),
            *[pltpu.VMEM((NBLK, BLOCK, COLS), F32)] * STEPS,
            pltpu.VMEM((2 * CHUNKS, NBLK, BLOCK, COLS), F32),
            pltpu.VMEM((STEPS, NBLK, BLOCK, COLS), F32),
            pltpu.VMEM((cols, 1, FACE), F32),
            pltpu.VMEM((1, FACE), F32),
            pltpu.VMEM((sums, 3, 1, COLS), F32),
            pltpu.VMEM((sums, rows, 3, 1, COLS), F32),
            pltpu.VMEM((sums, 3, 1, COLS), F32),
            pltpu.VMEM((sums, cols, 3, 1, COLS), F32),
            pltpu.SMEM((2, NBLK), jnp.int32),
            pltpu.SMEM((1, NBLK), jnp.int32),
            pltpu.SMEM((1, NBLK), jnp.int32),
            pltpu.VMEM((1, FACE), jnp.int32),
            pltpu.VMEM((ROUND, BLOCK, COLS), F32),
            pltpu.VMEM((ROUND, BLOCK, COLS), F32),
            dma((PIECES,)), dma((CHUNKS,)), dma((3,)),
            dma((2,)), dma((2,)), dma((3,)), dma((3,)), dma((2,)), dma((2,)), dma((STEPS,)), dma((STEPS,)),
            dma((2 * CHUNKS,)), dma((2 * CHUNKS,)),
            dma((STEPS, cols)), dma((STEPS, cols)),
            dma((cols,)), dma((cols,)),
            dma((sums, rows)), dma((sums, rows)),
            dma((sums, cols)), dma((sums, cols)),
        ],
        compiler_params=pltpu.CompilerParams(
            collective_id=0, has_side_effects=True, vmem_limit_bytes=54 * 2**20),
        cost_estimate=pl.CostEstimate(
            flops=3 * 6 * IFACE * IFACE * LOADS, bytes_accessed=4 * (IFACE * IFACE + IFACE * LOADS + 4 * FACE * LOADS),
            transcendentals=0),
    )(
        schur_matrix.reshape(IFACE, IFACE),
        load_vectors.reshape(IFACE, LOADS),
        glue_blocks.reshape(1, NBLK),
        contact_order.reshape(1, NBLK),
        active_flags.reshape(1, FACE),
    )
    outs = pl.pallas_call(
        hand_on,
        out_shape=[jax.ShapeDtypeStruct((FACE, LOADS), F32)] * 4,
        in_specs=[vmem] * 4,
        out_specs=[any_space] * 4,
        scratch_shapes=[dma((4,))],
        compiler_params=pltpu.CompilerParams(vmem_limit_bytes=4 * 2**20),
    )(*outs)
    return tuple(out[None, None] for out in outs)


def solution(mesh):
    return jax.shard_map(
        per_device,
        mesh=mesh,
        in_specs=(
            P("sub", "cont", None, None),
            P("sub", "cont", None, None),
            P("sub", "cont", None),
            P("sub", "cont", None),
            P("sub", "cont", None),
        ),
        out_specs=(P("sub", "cont", None, None),) * 4,
        check_vma=False,
    )
```
